32 devices in a mesh: aa: 4 (over x, core), ba: 8 (over z, y).
Axes of the slice: x: 2, y: 2, z: 4, core: 2. Of those that a mesh axis runs over, the one named last changes fastest.
Arguments:
- hidden: bfloat16 [512, 3072], P('aa'), may hold values from -24 to 24
- head_weight: bfloat16 [3072, 8, 4, 2048], P(None, 'ba'), as said below
- teacher: bfloat16 [512, 4, 8, 2048], P('ba', 'aa'), may hold values from -60 to 250
Outputs:
- divergence: float32 [], replicated
- grad_hidden: bfloat16 [512, 3072], P('aa')
- grad_head: bfloat16 [3072, 8, 4, 2048], P('aa', 'ba')
The draws below stay inside these ranges and needn't reach their ends.
Inputs may be any that keep to these rules, and one draw needn't show every extreme that they name: `head_weight`: entries of order one over the square root of 3072.
All inputs are finite; a program needn't handle non-finite values.
Results may differ from the reference program's by a relative error of at most 0.0049.
Values may be sent and summed in bfloat16 or wider, within the bound.
No kernel may reach another device: no remote copies, remote signals or barrier semaphores. Data moves between devices by JAX's collectives and lax.ppermute only.
A program may use at most 192 MiB of HBM per device.

```python
import math
import jax
import jax.numpy as jnp
from jax import lax

D = 3072
V = 65536
TOKENS = 512
VPIECE = 2048
N_AA = 4
N_BA = 8


def draw_hidden(key, part):
    values = jnp.clip(jax.random.normal(jax.random.fold_in(key, 31), (TOKENS, D), jnp.float32), -6.0, 6.0)
    return jnp.clip(values, -24.0, 24.0).astype(jnp.bfloat16)


def draw_head_weight(key, part):
    noise = jnp.clip(jax.random.normal(jax.random.fold_in(key, 41), (D, N_BA, N_AA, VPIECE), jnp.float32), -6.0, 6.0)
    spread = jnp.sqrt(1.0 + 2.2 * jnp.arange(N_BA, dtype=jnp.float32) / max(N_BA - 1, 1))
    weight = noise * spread[None, :, None, None] / math.sqrt(D)
    return weight.astype(jnp.bfloat16)


def draw_teacher(key, part):
    noise = jnp.clip(jax.random.normal(jax.random.fold_in(key, 51), (TOKENS, N_AA, N_BA, VPIECE), jnp.float32), -6.0, 6.0)
    rising = math.log(3.0) * jnp.arange(N_BA, dtype=jnp.float32) / max(N_BA - 1, 1)
    logits = 3.0 * noise + rising[None, None, :, None]
    return jnp.clip(logits, -60.0, 250.0).astype(jnp.bfloat16)


def setup_inputs(seed: int = 0) -> dict:
    key_of = jax.random.split(jax.random.key(seed), 4)
    hidden = draw_hidden(jax.random.fold_in(key_of[3], 71), 0)
    head_weight = draw_head_weight(jax.random.fold_in(key_of[3], 71), 0)
    teacher = draw_teacher(jax.random.fold_in(key_of[3], 71), 0)
    return {"hidden": hidden, "head_weight": head_weight, "teacher": teacher}


grad_scale = 256.0


def reference(hidden, head_weight, teacher):
    ordered = jnp.transpose(head_weight, (0, 2, 1, 3)).reshape(D, V)
    student = jnp.dot(hidden, ordered, preferred_element_type=jnp.float32)
    student_peak = jnp.max(student, axis=1, keepdims=True)
    student_total = jnp.sum(jnp.exp(student - student_peak), axis=1, keepdims=True)
    log_student = (student - student_peak) - jnp.log(student_total)
    target = teacher.reshape(TOKENS, V).astype(jnp.float32)
    target_peak = jnp.max(target, axis=1, keepdims=True)
    target_total = jnp.sum(jnp.exp(target - target_peak), axis=1, keepdims=True)
    log_target = (target - target_peak) - jnp.log(target_total)
    student_prob = jnp.exp(log_student)
    target_prob = jnp.exp(log_target)
    divergence = jnp.sum(target_prob * (log_target - log_student)) / TOKENS
    gradient = (grad_scale * (student_prob - target_prob)).astype(jnp.bfloat16)
    grad_hidden = lax.dot_general(gradient, ordered, (((1,), (1,)), ((), ())), preferred_element_type=jnp.float32).astype(jnp.bfloat16)
    grad_ordered = lax.dot_general(hidden, gradient, (((0,), (0,)), ((), ())), preferred_element_type=jnp.float32)
    grad_head = jnp.transpose(grad_ordered.reshape(D, N_AA, N_BA, VPIECE), (0, 2, 1, 3)).astype(jnp.bfloat16)
    return divergence, grad_hidden, grad_head
```

```python
import functools

import jax
import jax.numpy as jnp
from jax import lax
from jax.experimental import pallas as pl
from jax.experimental.pallas import tpu as pltpu
from jax.sharding import PartitionSpec as P

grad_scale = 256.0
lanes = 128
f32 = jnp.float32
bf16 = jnp.bfloat16
anywhere = pl.BlockSpec(memory_space=pl.ANY)
whole_vmem = pl.BlockSpec(memory_space=pltpu.VMEM)


def limits(mib):
    return pltpu.CompilerParams(vmem_limit_bytes=mib << 20)


def largest_tile(size, most, step):
    tile = min(size, most)
    while size % tile or tile % step:
        tile -= step
    return tile


def exchange(value, axis, mask):
    count = lax.axis_size(axis)
    return lax.ppermute(value, axis, [(i, i ^ mask) for i in range(count)])


def across(column, rows):
    del rows
    return jnp.transpose(jnp.broadcast_to(column, (lanes, column.shape[1])))


def split_teacher(teacher):
    tokens, _, owners, piece = teacher.shape
    cols = largest_tile(piece, 512, lanes)

    def kernel(in_ref, *refs):
        outs, stat_ref, peak_ref, total_ref = refs[:owners], refs[owners], refs[-2], refs[-1]
        step = pl.program_id(0)
        me = lax.axis_index("ba")
        flat = in_ref[:, 0].reshape(tokens * owners, cols)
        row = lax.broadcasted_iota(jnp.int32, (tokens * owners, tokens * owners), 0)
        col = lax.broadcasted_iota(jnp.int32, (tokens * owners, tokens * owners), 1)
        source = (row % tokens) * owners + ((row // tokens) ^ me)
        pick = (col == source).astype(f32).astype(bf16)
        moved = jnp.dot(pick, flat, preferred_element_type=f32)
        for s in range(owners):
            outs[s][...] = moved[s * tokens : (s + 1) * tokens].astype(bf16)
        parts = [
            moved[s * tokens : (s + 1) * tokens, k : k + lanes]
            for s in range(owners)
            for k in range(0, cols, lanes)
        ]
        peak = functools.reduce(jnp.maximum, parts)

        @pl.when(step == 0)
        def _():
            peak_ref[...] = peak
            total_ref[...] = jnp.zeros_like(total_ref)

        old = peak_ref[...]
        new = jnp.maximum(old, peak)
        total = total_ref[...] * jnp.exp(old - new)
        for part in parts:
            total = total + jnp.exp(part - new)
        peak_ref[...] = new
        total_ref[...] = total

        @pl.when(step == pl.num_programs(0) - 1)
        def _():
            top = jnp.max(new, axis=1, keepdims=True)
            summed = jnp.sum(total * jnp.exp(new - top), axis=1, keepdims=True)
            stat_ref[0:1, :] = jnp.transpose(jnp.broadcast_to(top, (tokens, lanes)))[0:1]
            stat_ref[1:2, :] = jnp.transpose(jnp.broadcast_to(summed, (tokens, lanes)))[0:1]
            stat_ref[2:8, :] = jnp.zeros((6, tokens), f32)

    return pl.pallas_call(
        kernel,
        grid=(piece // cols,),
        in_specs=[pl.BlockSpec((tokens, 1, owners, cols), lambda r: (0, 0, 0, r))],
        out_specs=[pl.BlockSpec((tokens, cols), lambda r: (0, r))] * owners
        + [pl.BlockSpec((8, tokens), lambda r: (0, 0))],
        out_shape=[jax.ShapeDtypeStruct((tokens, piece), bf16)] * owners
        + [jax.ShapeDtypeStruct((8, tokens), f32)],
        scratch_shapes=[pltpu.VMEM((tokens, lanes), f32)] * 2,
        compiler_params=limits(40),
        name="split_teacher",
    )(teacher)


def take_pair(head_weight):
    width, _, _, piece = head_weight.shape
    rows = largest_tile(width, 256, lanes)
    steps = width // rows

    def kernel(w_ref, out_ref, taken, ready, in_sem, out_sem):
        core = lax.axis_index("aa") % 2
        row = lax.broadcasted_iota(jnp.int32, (2 * lanes, 2 * lanes), 0)
        col = lax.broadcasted_iota(jnp.int32, (2 * lanes, 2 * lanes), 1)
        pick = (col == (row % lanes) * 2 + row // lanes).astype(f32).astype(bf16)

        def fetch(i, slot):
            at = pl.ds(pl.multiple_of(i * rows, rows), rows)
            return pltpu.make_async_copy(
                w_ref.at[at, 0, pl.ds(2 * core, 2), :], taken.at[slot], in_sem.at[slot]
            )

        def store(i, slot):
            at = pl.ds(pl.multiple_of(i * rows, rows), rows)
            return pltpu.make_async_copy(ready.at[slot], out_ref.at[:, at, :], out_sem.at[slot])

        fetch(0, 0).start()

        def body(i, carry):
            slot = lax.rem(i, 2)

            @pl.when(i + 1 < steps)
            def _():
                fetch(i + 1, 1 - slot).start()

            fetch(i, slot).wait()

            @pl.when(i >= 2)
            def _():
                store(i - 2, slot).wait()

            for q in range(0, rows, lanes):
                block = taken[slot, q : q + lanes].reshape(2 * lanes, piece)
                moved = jnp.dot(pick, block, preferred_element_type=f32).astype(bf16)
                ready[slot, 0, q : q + lanes] = moved[:lanes]
                ready[slot, 1, q : q + lanes] = moved[lanes:]
            store(i, slot).start()
            return carry

        lax.fori_loop(0, steps, body, 0)
        for i in range(max(0, steps - 2), steps):
            store(i, i % 2).wait()

    return pl.pallas_call(
        kernel,
        in_specs=[anywhere],
        out_specs=anywhere,
        out_shape=jax.ShapeDtypeStruct((2, width, piece), bf16),
        scratch_shapes=[
            pltpu.VMEM((2, rows, 2, piece), bf16),
            pltpu.VMEM((2, 2, rows, piece), bf16),
            pltpu.SemaphoreType.DMA((2,)),
            pltpu.SemaphoreType.DMA((2,)),
        ],
        compiler_params=limits(32),
        cost_estimate=pl.CostEstimate(
            flops=4 * lanes * 2 * width * piece, bytes_accessed=8 * width * piece, transcendentals=0
        ),
        name="take_pair",
    )(head_weight)


def student_logits(hiddens, pair):
    rows, width = hiddens[0].shape
    blocks = len(hiddens)
    tokens = rows * blocks
    piece = pair.shape[2]
    cols = largest_tile(piece, 512, lanes)

    def kernel(*refs):
        given, w_ref = refs[:blocks], refs[blocks]
        out_ref, stat_ref, left, peak_ref, total_ref, sem = refs[blocks + 1 :]
        first = (pl.program_id(0) == 0) & (pl.program_id(1) == 0)
        last = (pl.program_id(0) == 1) & (pl.program_id(1) == pl.num_programs(1) - 1)
        me = lax.axis_index("aa")

        @pl.when(first)
        def _():
            def place(q):
                at = pl.ds(pl.multiple_of((me ^ q) * rows, rows), rows)
                return pltpu.make_async_copy(given[q], left.at[at], sem.at[q])

            for q in range(blocks):
                place(q).start()
            peak_ref[...] = jnp.full_like(peak_ref, -jnp.inf)
            total_ref[...] = jnp.zeros_like(total_ref)
            for q in range(blocks):
                place(q).wait()

        out_ref[0] = jnp.dot(left[...], w_ref[0], preferred_element_type=f32)

        @pl.loop(0, tokens // 64)
        def _(k):
            at = pl.ds(pl.multiple_of(k * 64, 64), 64)
            parts = [out_ref[0, at, j : j + lanes] for j in range(0, cols, lanes)]
            old = peak_ref[at]
            new = functools.reduce(jnp.maximum, parts, old)
            total = total_ref[at] * jnp.exp(old - new)
            for part in parts:
                total = total + jnp.exp(part - new)
            peak_ref[at] = new
            total_ref[at] = total

        @pl.when(last)
        def _():
            peak = peak_ref[...]
            top = jnp.max(peak, axis=1, keepdims=True)
            summed = jnp.sum(total_ref[...] * jnp.exp(peak - top), axis=1, keepdims=True)
            stat_ref[0:1, :] = jnp.transpose(jnp.broadcast_to(top, (tokens, lanes)))[0:1]
            stat_ref[1:2, :] = jnp.transpose(jnp.broadcast_to(summed, (tokens, lanes)))[0:1]
            stat_ref[2:8, :] = jnp.zeros((6, tokens), f32)

    return pl.pallas_call(
        kernel,
        grid=(2, piece // cols),
        in_specs=[anywhere] * blocks + [pl.BlockSpec((1, width, cols), lambda i, r: (i, 0, r))],
        out_specs=[
            pl.BlockSpec((1, tokens, cols), lambda i, r: (i, 0, r)),
            pl.BlockSpec((8, tokens), lambda i, r: (0, 0)),
        ],
        out_shape=[
            jax.ShapeDtypeStruct((2, tokens, piece), f32),
            jax.ShapeDtypeStruct((8, tokens), f32),
        ],
        scratch_shapes=[
            pltpu.VMEM((tokens, width), bf16),
            pltpu.VMEM((tokens, lanes), f32),
            pltpu.VMEM((tokens, lanes), f32),
            pltpu.SemaphoreType.DMA((blocks,)),
        ],
        compiler_params=limits(40),
        cost_estimate=pl.CostEstimate(
            flops=4 * tokens * width * piece, bytes_accessed=4 * width * piece, transcendentals=0
        ),
        name="student_logits",
    )(*hiddens, pair)


def merge(stats):
    peak = functools.reduce(jnp.maximum, [s[0:1] for s in stats])
    total = sum(s[1:2] * jnp.exp(s[0:1] - peak) for s in stats)
    return peak, total


def pack_stats(student_stats, teacher_stats):
    tokens = student_stats[0].shape[1]
    few = teacher_stats[0].shape[1]
    count = len(student_stats)

    def kernel(*refs):
        out_ref = refs[-1]
        peak, total = merge([r[...] for r in refs[:count]])
        out_ref[0:1, :] = peak
        out_ref[1:2, :] = total
        out_ref[2:8, :] = jnp.zeros((6, tokens), f32)
        peak, total = merge([r[...] for r in refs[count:-1]])
        out_ref[2:3, 0:few] = peak + jnp.log(total)

    return pl.pallas_call(
        kernel,
        in_specs=[whole_vmem] * (count + len(teacher_stats)),
        out_specs=whole_vmem,
        out_shape=jax.ShapeDtypeStruct((8, tokens), f32),
        name="pack_stats",
    )(*student_stats, *teacher_stats)


def all_log_sums(packed, few):
    count = len(packed)
    tokens = packed[0].shape[1]

    def kernel(*refs):
        student_ref, teacher_ref = refs[count:]
        me = lax.axis_index("ba")
        peak, total = merge([r[...] for r in refs[:count]])
        student_ref[...] = across(peak + jnp.log(total), tokens)
        for s in range(count):
            at = pl.ds(pl.multiple_of((me ^ s) * few, few), few)
            wide = jnp.broadcast_to(refs[s][2:3, 0:lanes], (lanes, lanes))
            teacher_ref[at, :] = jnp.transpose(wide)[0:few]

    return pl.pallas_call(
        kernel,
        in_specs=[whole_vmem] * count,
        out_specs=[whole_vmem] * 2,
        out_shape=[jax.ShapeDtypeStruct((tokens, lanes), f32)] * 2,
        name="all_log_sums",
    )(*packed)


def logit_gradient(order, own, met, student, student_sum, teacher_sum):
    count = order.shape[0] - 1
    _, tokens, piece = student.shape
    few = own.shape[0] // count
    cols = largest_tile(piece, 512, lanes)
    rows = 16
    half = tokens // 2

    def kernel(order_ref, own_ref, met_ref, s_ref, ssum_ref, tsum_ref, g_ref, div_ref):
        step = pl.program_id(0)
        x = order_ref[count]

        @pl.when(step == 0)
        def _():
            div_ref[...] = jnp.zeros_like(div_ref)

        mine = (order_ref[step] * few) // half == x
        counted = jnp.where(mine, 1.0, 0.0)

        @pl.loop(0, few // rows)
        def _(k):
            at = pl.ds(pl.multiple_of(k * rows, rows), rows)
            ssum = ssum_ref[at]
            tsum = tsum_ref[at]
            ssum = jnp.concatenate([ssum] * (cols // lanes), axis=1)
            tsum = jnp.concatenate([tsum] * (cols // lanes), axis=1)
            found = jnp.zeros((8, lanes), f32)
            for which, t_ref in ((x, own_ref), (1 - x, met_ref)):
                for j in range(0, piece, cols):
                    log_s = s_ref[which, at, j : j + cols] - ssum
                    log_t = t_ref[at, j : j + cols].astype(f32) - tsum
                    prob_t = jnp.exp(log_t)
                    g_ref[which, at, j : j + cols] = (
                        grad_scale * (jnp.exp(log_s) - prob_t)
                    ).astype(bf16)
                    part = prob_t * (log_t - log_s)
                    for m in range(0, rows, 8):
                        for n in range(0, cols, lanes):
                            found = found + part[m : m + 8, n : n + lanes]
            div_ref[...] += counted * found

    return pl.pallas_call(
        kernel,
        grid_spec=pltpu.PrefetchScalarGridSpec(
            num_scalar_prefetch=1,
            grid=(count,),
            in_specs=[
                pl.BlockSpec((few, piece), lambda s, o: (s, 0)),
                pl.BlockSpec((few, piece), lambda s, o: (s, 0)),
                pl.BlockSpec((2, few, piece), lambda s, o: (0, o[s], 0)),
                pl.BlockSpec((few, lanes), lambda s, o: (o[s], 0)),
                pl.BlockSpec((few, lanes), lambda s, o: (o[s], 0)),
            ],
            out_specs=[
                pl.BlockSpec((2, few, piece), lambda s, o: (0, o[s], 0)),
                pl.BlockSpec((8, lanes), lambda s, o: (0, 0)),
            ],
        ),
        out_shape=[
            jax.ShapeDtypeStruct((2, tokens, piece), bf16),
            jax.ShapeDtypeStruct((8, lanes), f32),
        ],
        compiler_params=limits(32),
        name="logit_gradient",
    )(order, own, met, student, student_sum, teacher_sum)


def hidden_share(position, gradient, pair):
    _, tokens, piece = gradient.shape
    width = pair.shape[1]
    rows = tokens // lax.axis_size("aa")
    cols = largest_tile(width, 384, lanes)

    def kernel(at_ref, keep_ref, send_ref, w_ref, kept_ref, sent_ref):
        total = jnp.zeros((2 * rows, cols), f32)
        for i in range(2):
            left = jnp.concatenate([keep_ref[i], send_ref[i]], axis=0)
            total = total + lax.dot_general(
                left, w_ref[i], (((1,), (1,)), ((), ())), preferred_element_type=f32
            )
        kept_ref[...] = total[:rows]
        sent_ref[...] = total[rows:].astype(bf16)

    return pl.pallas_call(
        kernel,
        grid_spec=pltpu.PrefetchScalarGridSpec(
            num_scalar_prefetch=1,
            grid=(width // cols,),
            in_specs=[
                pl.BlockSpec((2, rows, piece), lambda d, p: (0, p[0], 0)),
                pl.BlockSpec((2, rows, piece), lambda d, p: (0, p[1], 0)),
                pl.BlockSpec((2, cols, piece), lambda d, p: (0, d, 0)),
            ],
            out_specs=[pl.BlockSpec((rows, cols), lambda d, p: (0, d))] * 2,
        ),
        out_shape=[
            jax.ShapeDtypeStruct((rows, width), f32),
            jax.ShapeDtypeStruct((rows, width), bf16),
        ],
        compiler_params=limits(32),
        cost_estimate=pl.CostEstimate(
            flops=8 * rows * width * piece, bytes_accessed=4 * width * piece, transcendentals=0
        ),
        name="hidden_share",
    )(position, gradient, gradient, pair)


def share_out(kept, arrived):
    rows, width = kept.shape
    count = lax.axis_size("ba")
    few = rows // count
    if few % 16:
        order = lax.axis_index("ba") ^ jnp.arange(count)
        summed = (kept + arrived.astype(f32)).astype(bf16).reshape(count, few, width)
        return [summed[order[s]] for s in range(count)]

    def kernel(kept_ref, arrived_ref, *outs):
        me = lax.axis_index("ba")
        for s in range(count):
            at = pl.ds(pl.multiple_of((me ^ s) * few, few), few)
            outs[s][...] = (kept_ref[at] + arrived_ref[at].astype(f32)).astype(bf16)

    return pl.pallas_call(
        kernel,
        in_specs=[whole_vmem] * 2,
        out_specs=[whole_vmem] * count,
        out_shape=[jax.ShapeDtypeStruct((few, width), bf16)] * count,
        name="share_out",
    )(kept, arrived)


def put_together(blocks):
    count = len(blocks)
    few, width = blocks[0].shape
    if few % 16:
        order = lax.axis_index("ba") ^ jnp.arange(count)
        return jnp.stack(blocks)[order].reshape(count * few, width)

    def kernel(*refs):
        me = lax.axis_index("ba")
        for s in range(count):
            at = pl.ds(pl.multiple_of((me ^ s) * few, few), few)
            refs[count][at, :] = refs[s][...]

    return pl.pallas_call(
        kernel,
        in_specs=[whole_vmem] * count,
        out_specs=whole_vmem,
        out_shape=jax.ShapeDtypeStruct((count * few, width), bf16),
        name="put_together",
    )(*blocks)


def head_pair(hiddens, gradient, other, so_far):
    rows, width = hiddens[0].shape
    blocks = len(hiddens)
    tokens = rows * blocks
    piece = gradient.shape[2]
    share = width // blocks
    cols = largest_tile(piece, 512, lanes)
    steps = piece // cols
    aliased = [] if so_far is None else [so_far]

    def kernel(*refs):
        given, g_ref = refs[:blocks], refs[blocks]
        out_ref, held, left, ready, sem, out_sem = refs[blocks + 1 + len(aliased) :]
        step = pl.program_id(0)
        slot = lax.rem(step, 2)
        me = lax.axis_index("aa")
        base = 2 * ((me % 2) ^ other)

        @pl.when(step == 0)
        def _():
            def place(q):
                at = pl.ds(pl.multiple_of((me ^ q) * rows, rows), rows)
                part = pl.ds(pl.multiple_of(me * share, share), share)
                return pltpu.make_async_copy(given[q].at[:, part], held.at[at], sem.at[q])

            for q in range(blocks):
                place(q).start()
            for q in range(blocks):
                place(q).wait()
            row = lax.broadcasted_iota(jnp.int32, (2 * lanes, lanes), 0)
            col = lax.broadcasted_iota(jnp.int32, (2 * lanes, lanes), 1)
            for i in range(2):
                spread = (row == 2 * col + i).astype(f32).astype(bf16)
                for d in range(0, share, lanes):
                    left[2 * d : 2 * (d + lanes), i * tokens : (i + 1) * tokens] = lax.dot_general(
                        spread,
                        held[:, d : d + lanes],
                        (((1,), (1,)), ((), ())),
                        preferred_element_type=f32,
                    ).astype(bf16)

        def store(k, s):
            at = pl.ds(pl.multiple_of(k * cols, cols), cols)
            return pltpu.make_async_copy(
                ready.at[s], out_ref.at[:, 0, pl.ds(base, 2), at], out_sem.at[s]
            )

        @pl.when(step >= 2)
        def _():
            store(step - 2, slot).wait()

        right = g_ref[...].reshape(2 * tokens, cols)
        for d in range(0, 2 * share, 512):
            made = jnp.dot(left[d : d + 512], right, preferred_element_type=f32).astype(bf16)
            ready[slot, d // 2 : d // 2 + 256] = made.reshape(256, 2, cols)
        store(step, slot).start()

        @pl.when(step == steps - 1)
        def _():
            if steps > 1:
                store(step - 1, 1 - slot).wait()
            store(step, slot).wait()

    return pl.pallas_call(
        kernel,
        grid=(steps,),
        in_specs=[anywhere] * blocks
        + [pl.BlockSpec((2, tokens, cols), lambda r: (0, 0, r))]
        + [anywhere] * len(aliased),
        out_specs=anywhere,
        out_shape=jax.ShapeDtypeStruct((share, 1, 4, piece), bf16),
        scratch_shapes=[
            pltpu.VMEM((tokens, share), bf16),
            pltpu.VMEM((2 * share, 2 * tokens), bf16),
            pltpu.VMEM((2, share, 2, cols), bf16),
            pltpu.SemaphoreType.DMA((blocks,)),
            pltpu.SemaphoreType.DMA((2,)),
        ],
        input_output_aliases={blocks + 1: 0} if aliased else {},
        compiler_params=limits(40),
        cost_estimate=pl.CostEstimate(
            flops=8 * share * tokens * piece, bytes_accessed=4 * share * piece, transcendentals=0
        ),
        name="head_pair",
    )(*hiddens, gradient, *aliased)


def on_device(hidden, head_weight, teacher):
    me_a = lax.axis_index("aa")
    me_b = lax.axis_index("ba")
    count = lax.axis_size("ba")
    few = teacher.shape[0]
    tokens = few * count
    x = me_a // 2

    side = exchange(hidden, "aa", 2)
    core = exchange(hidden, "aa", 1)
    hiddens = [hidden, core, side, exchange(side, "aa", 1)]

    *blocks, teacher_stat = split_teacher(teacher)
    arrived = [blocks[0]] + [exchange(blocks[s], "ba", s) for s in range(1, count)]
    teacher_stats = [teacher_stat] + [exchange(teacher_stat, "aa", m) for m in (1, 2, 3)]

    pair = take_pair(head_weight)
    student, student_stat = student_logits(hiddens, pair)
    packed = pack_stats([student_stat, exchange(student_stat, "aa", 1)], teacher_stats)
    packed = [packed] + [exchange(packed, "ba", s) for s in range(1, count)]
    student_sum, teacher_sum = all_log_sums(packed, few)

    mine = jnp.concatenate(arrived, axis=0)
    met = lax.ppermute(mine, "aa", [(0, 2), (3, 1), (1, 0), (2, 3)])
    own = lax.ppermute(mine, "aa", [(0, 0), (1, 2), (2, 1), (3, 3)])
    order = jnp.concatenate([me_b ^ jnp.arange(count), x[None]]).astype(jnp.int32)
    gradient, found = logit_gradient(order, own, met, student, student_sum, teacher_sum)

    position = jnp.stack([me_a, me_a ^ 1]).astype(jnp.int32)
    kept, sent = hidden_share(position, gradient, pair)
    shares = share_out(kept, exchange(sent, "aa", 1))
    summed = shares[0].astype(f32)
    for s in range(1, count):
        summed = summed + exchange(shares[s], "ba", s).astype(f32)
    summed = summed.astype(bf16)
    grad_hidden = put_together([summed] + [exchange(summed, "ba", s) for s in range(1, count)])

    other = exchange(gradient, "aa", 1)
    grad_head = head_pair(hiddens, gradient, 0, None)
    grad_head = head_pair(hiddens, other, 1, grad_head)

    divergence = jnp.sum(found)[None]
    mask = 1
    while mask < lax.axis_size("aa"):
        divergence = divergence + exchange(divergence, "aa", mask)
        mask *= 2
    mask = 1
    while mask < count:
        divergence = divergence + exchange(divergence, "ba", mask)
        mask *= 2
    return divergence[0] / tokens, grad_hidden, grad_head


def solution(mesh):
    placed = (P("aa", None), P(None, "ba", None, None), P("ba", "aa", None, None))
    return jax.shard_map(
        on_device,
        mesh=mesh,
        in_specs=placed,
        out_specs=(P(), P("aa", None), P("aa", "ba", None, None)),
        check_vma=False,
    )
```

```python
import functools

import jax
import jax.numpy as jnp
from jax import lax
from jax.experimental import pallas as pl
from jax.experimental.pallas import tpu as pltpu
from jax.sharding import PartitionSpec as P

grad_scale = 256.0
lanes = 128
absent = -1e30
f32 = jnp.float32
bf16 = jnp.bfloat16
anywhere = pl.BlockSpec(memory_space=pl.ANY)
whole_vmem = pl.BlockSpec(memory_space=pltpu.VMEM)


def in_hbm(*values):
    return [pltpu.with_memory_space_constraint(value, pltpu.HBM) for value in values]


def in_vmem(value):
    return pltpu.with_memory_space_constraint(value, pltpu.VMEM)


def limits(mib):
    return pltpu.CompilerParams(vmem_limit_bytes=mib << 20)


def largest_tile(size, most, step):
    tile = min(size, most)
    while size % tile or tile % step:
        tile -= step
    return tile


def my_pair():
    me = lax.axis_index("aa")
    return (me % 2) ^ (me // 2)


def gate(values, deps):
    return lax.optimization_barrier((values, deps))[0]


def exchange(value, axis, mask):
    count = lax.axis_size(axis)
    return lax.ppermute(value, axis, [(i, i ^ mask) for i in range(count)])


def lane_row(column, rows):
    return jnp.transpose(jnp.broadcast_to(column, (rows, lanes)))[0:1]


def split_teacher(teacher):
    tokens, _, owners, piece = teacher.shape
    every = tokens * owners
    cols = largest_tile(piece, 512, lanes)

    def kernel(in_ref, *refs):
        outs, (stat_ref, peak_ref, total_ref) = refs[:owners], refs[owners:]
        step = pl.program_id(0)
        me = lax.axis_index("ba")
        flat = in_ref[:, 0].reshape(every, cols)
        row = lax.broadcasted_iota(jnp.int32, (every, every), 0)
        col = lax.broadcasted_iota(jnp.int32, (every, every), 1)
        source = (row % tokens) * owners + ((row // tokens) ^ me)
        pick = (col == source).astype(f32).astype(bf16)
        moved = jnp.dot(pick, flat, preferred_element_type=f32)
        for s in range(owners):
            outs[s][...] = moved[s * tokens : (s + 1) * tokens].astype(bf16)
        parts = [
            moved[s * tokens : (s + 1) * tokens, k : k + lanes]
            for s in range(owners)
            for k in range(0, cols, lanes)
        ]
        peak = functools.reduce(jnp.maximum, parts)

        @pl.when(step == 0)
        def _():
            peak_ref[...] = peak
            total_ref[...] = jnp.zeros_like(total_ref)

        old = peak_ref[...]
        new = jnp.maximum(old, peak)
        total = total_ref[...] * jnp.exp(old - new)
        for part in parts:
            total = total + jnp.exp(part - new)
        peak_ref[...] = new
        total_ref[...] = total

        @pl.when(step == pl.num_programs(0) - 1)
        def _():
            top = jnp.max(new, axis=1, keepdims=True)
            summed = jnp.sum(total * jnp.exp(new - top), axis=1, keepdims=True)
            token = lax.broadcasted_iota(jnp.int32, (tokens, every), 0) + me * tokens
            here = token == lax.broadcasted_iota(jnp.int32, (tokens, every), 1)
            peaks = jnp.max(jnp.where(here, top, absent), axis=0, keepdims=True)
            sums = jnp.sum(jnp.where(here, summed, 0.0), axis=0, keepdims=True)
            stat_ref[0:1, :] = peaks
            stat_ref[1:2, :] = sums
            stat_ref[2:8, :] = jnp.zeros((6, every), f32)

    return pl.pallas_call(
        kernel,
        grid=(piece // cols,),
        in_specs=[pl.BlockSpec((tokens, 1, owners, cols), lambda r: (0, 0, 0, r))],
        out_specs=[pl.BlockSpec((tokens, cols), lambda r: (0, r))] * owners
        + [pl.BlockSpec((8, every), lambda r: (0, 0))],
        out_shape=[pltpu.HBM((tokens, piece), bf16)] * owners
        + [jax.ShapeDtypeStruct((8, every), f32)],
        scratch_shapes=[pltpu.VMEM((tokens, lanes), f32)] * 2,
        compiler_params=limits(20),
        name="split_teacher",
    )(*in_hbm(teacher))


def take_pair(head_weight):
    width, _, _, piece = head_weight.shape
    rows = largest_tile(width, 256, lanes)
    steps = width // rows
    depth = min(4, steps)

    def kernel(w_ref, out_ref, taken, in_sem):
        pair = my_pair()
        row = lax.broadcasted_iota(jnp.int32, (2 * lanes, 2 * lanes), 0)
        col = lax.broadcasted_iota(jnp.int32, (2 * lanes, 2 * lanes), 1)
        pick = (col == (row % lanes) * 2 + row // lanes).astype(f32).astype(bf16)

        def fetch(i):
            return pltpu.make_async_copy(
                w_ref.at[pl.ds(i * rows, rows), 0, pl.ds(2 * pair, 2), :],
                taken.at[i % depth],
                in_sem.at[i % depth],
            )

        for i in range(depth):
            fetch(i).start()
        for i in range(steps):
            fetch(i).wait()
            for q in range(0, rows, lanes):
                block = taken[i % depth, q : q + lanes].reshape(2 * lanes, piece)
                moved = jnp.dot(pick, block, preferred_element_type=f32).astype(bf16)
                at = i * rows + q
                out_ref[0, at : at + lanes] = moved[:lanes]
                out_ref[1, at : at + lanes] = moved[lanes:]
            if i + depth < steps:
                fetch(i + depth).start()

    return pl.pallas_call(
        kernel,
        in_specs=[anywhere],
        out_specs=whole_vmem,
        out_shape=pltpu.VMEM((2, width, piece), bf16),
        scratch_shapes=[
            pltpu.VMEM((depth, rows, 2, piece), bf16),
            pltpu.SemaphoreType.DMA((depth,)),
        ],
        compiler_params=limits(20),
        cost_estimate=pl.CostEstimate(
            flops=16 * lanes * width * piece,
            bytes_accessed=4 * width * piece,
            transcendentals=0,
        ),
        name="take_pair",
    )(head_weight)


def student_logits(hiddens, pair, which):
    rows, width = hiddens[0].shape
    blocks = len(hiddens)
    tokens = rows * blocks
    piece = pair.shape[2]
    cols = largest_tile(piece, 512, lanes)

    def kernel(*refs):
        given, w_ref = refs[:blocks], refs[blocks]
        out_ref, stat_ref, left, peak_ref, total_ref, sem = refs[blocks + 1 :]
        step = pl.program_id(0)
        me = lax.axis_index("aa")

        @pl.when(step == 0)
        def _():
            def place(q):
                at = pl.ds(pl.multiple_of((me ^ q) * rows, rows), rows)
                return pltpu.make_async_copy(given[q], left.at[at], sem.at[q])

            for q in range(blocks):
                place(q).start()
            peak_ref[...] = jnp.full_like(peak_ref, absent)
            total_ref[...] = jnp.zeros_like(total_ref)
            for q in range(blocks):
                place(q).wait()

        at = pl.ds(pl.multiple_of(step * cols, cols), cols)
        out_ref[...] = jnp.dot(left[...], w_ref[which, :, at], preferred_element_type=f32)

        @pl.loop(0, tokens // 64)
        def _(k):
            at = pl.ds(pl.multiple_of(k * 64, 64), 64)
            parts = [out_ref[at, j : j + lanes] for j in range(0, cols, lanes)]
            old = peak_ref[at]
            new = functools.reduce(jnp.maximum, parts, old)
            total = total_ref[at] * jnp.exp(old - new)
            for part in parts:
                total = total + jnp.exp(part - new)
            peak_ref[at] = new
            total_ref[at] = total

        @pl.when(step == pl.num_programs(0) - 1)
        def _():
            peak = peak_ref[...]
            top = jnp.max(peak, axis=1, keepdims=True)
            summed = jnp.sum(total_ref[...] * jnp.exp(peak - top), axis=1, keepdims=True)
            stat_ref[0:1, :] = lane_row(top, tokens)
            stat_ref[1:2, :] = lane_row(summed, tokens)
            stat_ref[2:8, :] = jnp.zeros((6, tokens), f32)

    return pl.pallas_call(
        kernel,
        grid=(piece // cols,),
        in_specs=[anywhere] * blocks
        + [whole_vmem],
        out_specs=[
            pl.BlockSpec((tokens, cols), lambda r: (0, r)),
            pl.BlockSpec((8, tokens), lambda r: (0, 0)),
        ],
        out_shape=[
            pltpu.HBM((tokens, piece), f32),
            jax.ShapeDtypeStruct((8, tokens), f32),
        ],
        scratch_shapes=[
            pltpu.VMEM((tokens, width), bf16),
            pltpu.VMEM((tokens, lanes), f32),
            pltpu.VMEM((tokens, lanes), f32),
            pltpu.SemaphoreType.DMA((blocks,)),
        ],
        compiler_params=limits(20),
        cost_estimate=pl.CostEstimate(flops=1, bytes_accessed=1, transcendentals=0),
        name="student_logits",
    )(*in_hbm(*hiddens), in_vmem(pair))


def merge(stats, row=0):
    peak = functools.reduce(jnp.maximum, [s[row : row + 1] for s in stats])
    total = sum(s[row + 1 : row + 2] * jnp.exp(s[row : row + 1] - peak) for s in stats)
    return peak, total


def pack_stats(student_stats, teacher_stats):
    tokens = student_stats[0].shape[1]
    count = len(student_stats)

    def kernel(*refs):
        out_ref = refs[-1]
        peak, total = merge([r[...] for r in refs[:count]])
        out_ref[0:1, :] = peak
        out_ref[1:2, :] = total
        peak, total = merge([r[...] for r in refs[count:-1]])
        out_ref[2:3, :] = peak
        out_ref[3:4, :] = total
        out_ref[4:8, :] = jnp.zeros((4, tokens), f32)

    return pl.pallas_call(
        kernel,
        in_specs=[whole_vmem] * (count + len(teacher_stats)),
        out_specs=whole_vmem,
        out_shape=jax.ShapeDtypeStruct((8, tokens), f32),
        compiler_params=limits(20),
        name="pack_stats",
    )(*student_stats, *teacher_stats)


def merge_two(first, second):
    tokens = first.shape[1]

    def kernel(a_ref, b_ref, out_ref):
        both = [a_ref[...], b_ref[...]]
        for row in (0, 2):
            peak, total = merge(both, row)
            out_ref[row : row + 1, :] = peak
            out_ref[row + 1 : row + 2, :] = total
        out_ref[4:8, :] = jnp.zeros((4, tokens), f32)

    return pl.pallas_call(
        kernel,
        in_specs=[whole_vmem] * 2,
        out_specs=whole_vmem,
        out_shape=jax.ShapeDtypeStruct((8, tokens), f32),
        compiler_params=limits(20),
        name="merge_two",
    )(first, second)


def all_log_sums(first, second):
    tokens = first.shape[1]

    def kernel(a_ref, b_ref, *outs):
        both = [a_ref[...], b_ref[...]]
        for row, out_ref in zip((0, 2), outs):
            peak, total = merge(both, row)
            wide = jnp.broadcast_to(peak + jnp.log(total), (lanes, tokens))
            out_ref[...] = jnp.transpose(wide)

    return pl.pallas_call(
        kernel,
        in_specs=[whole_vmem] * 2,
        out_specs=[whole_vmem] * 2,
        out_shape=[pltpu.HBM((tokens, lanes), f32)] * 2,
        compiler_params=limits(20),
        name="all_log_sums",
    )(first, second)


def logit_gradient(plan, groups, students, student_sum, teacher_sum):
    kinds = len(groups)
    count = (plan.shape[0] - 1) // (3 + kinds)
    tokens, piece = students[0].shape
    half = tokens // 2
    few = half // count
    cols = largest_tile(piece, 512, lanes)
    rows = 16

    def kernel(plan_ref, *refs):
        teachers, s_refs = refs[: 4 * kinds], refs[4 * kinds : 4 * kinds + 2]
        ssum_ref, tsum_ref = refs[4 * kinds + 2 : 4 * kinds + 4]
        g_ref, div_ref = refs[-2:]
        step = pl.program_id(0)
        kind = plan_ref[(2 + kinds) * count + step]
        core = plan_ref[(3 + kinds) * count]

        @pl.when(step == 0)
        def _():
            div_ref[...] = jnp.zeros_like(div_ref)

        def work(ordered):
            @pl.loop(0, few // rows)
            def _(k):
                at = pl.ds(pl.multiple_of(k * rows, rows), rows)
                ssum = jnp.concatenate([ssum_ref[at]] * (cols // lanes), axis=1)
                tsum = jnp.concatenate([tsum_ref[at]] * (cols // lanes), axis=1)
                found = jnp.zeros((rows, cols), f32)
                for i, t_ref in enumerate(ordered):
                    for j in range(0, piece, cols):
                        log_s = s_refs[i][at, j : j + cols] - ssum
                        log_t = t_ref[at, j : j + cols].astype(f32) - tsum
                        prob_t = jnp.exp(log_t)
                        g_ref[i, at, j : j + cols] = (
                            grad_scale * (jnp.exp(log_s) - prob_t)
                        ).astype(bf16)
                        found = found + prob_t * (log_t - log_s)
                folded = [
                    found[m : m + 8, n : n + lanes]
                    for m in range(0, rows, 8)
                    for n in range(0, cols, lanes)
                ]
                div_ref[...] += sum(folded[1:], folded[0])

        for at_kind in range(kinds):
            for at_core in (0, 1):
                own_ref, side_ref, own_met_ref, side_met_ref = teachers[4 * at_kind : 4 * at_kind + 4]

                @pl.when((kind == at_kind) & (core == at_core))
                def _(ordered=((own_ref, own_met_ref), (side_met_ref, side_ref))[at_core]):
                    work(ordered)

    def block_of(kind, of_core):
        def at(s, p):
            return (jnp.where(p[(3 + kinds) * count] == of_core, p[(2 + kind) * count + s], 0), 0)

        return at

    return pl.pallas_call(
        kernel,
        grid_spec=pltpu.PrefetchScalarGridSpec(
            num_scalar_prefetch=1,
            grid=(count,),
            in_specs=[
                pl.BlockSpec((few, piece), block_of(kind, n % 2)) for kind in range(kinds) for n in range(4)
            ]
            + [pl.BlockSpec((few, piece), lambda s, p: (p[count + s], 0))] * 2
            + [pl.BlockSpec((few, lanes), lambda s, p: (p[count + s], 0))] * 2,
            out_specs=[
                pl.BlockSpec((2, few, piece), lambda s, p: (0, p[s], 0)),
                pl.BlockSpec((8, lanes), lambda s, p: (0, 0)),
            ],
        ),
        out_shape=[
            pltpu.HBM((2, half, piece), bf16),
            jax.ShapeDtypeStruct((8, lanes), f32),
        ],
        compiler_params=limits(20),
        cost_estimate=pl.CostEstimate(
            flops=8 * half * piece, bytes_accessed=16 * half * piece, transcendentals=4 * half * piece
        ),
        name="logit_gradient",
    )(
        plan,
        *in_hbm(*[part for group in groups for part in group]),
        *in_hbm(*students, student_sum, teacher_sum),
    )


def hidden_share(gradient, pair):
    _, tokens, piece = gradient.shape
    width = pair.shape[1]
    half = tokens // 2
    cols = largest_tile(width, 768, lanes)

    def kernel(g_ref, w_ref, kept_ref, sent_ref):
        core = lax.axis_index("aa") % 2
        total = sum(
            lax.dot_general(
                g_ref[i], w_ref[i], (((1,), (1,)), ((), ())), preferred_element_type=f32
            )
            for i in range(2)
        )

        @pl.when(core == 0)
        def _():
            kept_ref[...] = total[:half]
            sent_ref[...] = total[half:].astype(bf16)

        @pl.when(core == 1)
        def _():
            kept_ref[...] = total[half:]
            sent_ref[...] = total[:half].astype(bf16)

    return pl.pallas_call(
        kernel,
        grid=(width // cols,),
        in_specs=[
            pl.BlockSpec((2, tokens, piece), lambda d: (0, 0, 0)),
            pl.BlockSpec((2, cols, piece), lambda d: (0, d, 0)),
        ],
        out_specs=[pl.BlockSpec((half, cols), lambda d: (0, d))] * 2,
        out_shape=[
            jax.ShapeDtypeStruct((half, width), f32),
            jax.ShapeDtypeStruct((half, width), bf16),
        ],
        compiler_params=limits(40),
        cost_estimate=pl.CostEstimate(
            flops=4 * tokens * width * piece, bytes_accessed=4 * width * piece, transcendentals=0
        ),
        name="hidden_share",
    )(*in_hbm(gradient, pair))


def three_parts(value):
    high = lax.reduce_precision(value, 8, 7)
    rest = value - high
    middle = lax.reduce_precision(rest, 8, 7)
    return high, middle, rest - middle


def share_out(kept, arrived, found):
    rows, width = kept.shape
    count = lax.axis_size("ba")
    few = rows // count
    if few % 16:
        order = lax.axis_index("ba") ^ jnp.arange(count)
        summed = (kept + arrived.astype(f32)).astype(bf16).reshape(count, few, width)
        parts = jnp.stack(three_parts(jnp.sum(found))).astype(bf16)
        carried = jnp.zeros((few, lanes), bf16).at[0, :3].set(parts)
        return [jnp.concatenate([summed[order[s]], carried], axis=1) for s in range(count)]

    def kernel(kept_ref, arrived_ref, found_ref, *outs):
        me = lax.axis_index("ba")
        total = jnp.sum(found_ref[...], axis=0, keepdims=True)
        total = jnp.sum(total, axis=1, keepdims=True)
        high = total.astype(bf16).astype(f32)
        middle = (total - high).astype(bf16).astype(f32)
        low = total - high - middle
        lane = lax.broadcasted_iota(jnp.int32, (few, lanes), 1)
        lane = lane + lanes * lax.broadcasted_iota(jnp.int32, (few, lanes), 0)
        carried = jnp.where(lane == 0, high, jnp.where(lane == 1, middle, jnp.where(lane == 2, low, 0.0)))
        for s in range(count):
            at = pl.ds(pl.multiple_of((me ^ s) * few, few), few)
            outs[s][:, :width] = (kept_ref[at] + arrived_ref[at].astype(f32)).astype(bf16)
            outs[s][:, width:] = carried.astype(bf16)

    return pl.pallas_call(
        kernel,
        in_specs=[whole_vmem] * 3,
        out_specs=[whole_vmem] * count,
        out_shape=[jax.ShapeDtypeStruct((few, width + lanes), bf16)] * count,
        compiler_params=limits(20),
        name="share_out",
    )(kept, arrived, found)


def put_together(blocks):
    count = len(blocks)
    few, width = blocks[0].shape
    if few % 16:
        order = lax.axis_index("ba") ^ jnp.arange(count)
        return jnp.stack(blocks)[order].reshape(count * few, width)

    def kernel(*refs):
        me = lax.axis_index("ba")
        for s in range(count):
            at = pl.ds(pl.multiple_of((me ^ s) * few, few), few)
            refs[count][at, :] = refs[s][...]

    return pl.pallas_call(
        kernel,
        in_specs=[whole_vmem] * count,
        out_specs=whole_vmem,
        out_shape=jax.ShapeDtypeStruct((count * few, width), bf16),
        compiler_params=limits(20),
        name="put_together",
    )(*blocks)


def spread_features(hiddens):
    rows, width = hiddens[0].shape
    blocks = len(hiddens)
    tokens = rows * blocks
    share = width // blocks

    def kernel(*refs):
        given = refs[:blocks]
        left, held, sem = refs[blocks:]
        me = lax.axis_index("aa")
        def place(q):
            block = q // 2 * 2 + ((me % 2) ^ (q % 2))
            at = pl.ds(pl.multiple_of(block * rows, rows), rows)
            part = pl.ds(pl.multiple_of(me * share, share), share)
            return pltpu.make_async_copy(given[q].at[:, part], held.at[at], sem.at[q])

        for q in range(blocks):
            place(q).start()
        for q in range(blocks):
            place(q).wait()
        row = lax.broadcasted_iota(jnp.int32, (2 * lanes, lanes), 0)
        col = lax.broadcasted_iota(jnp.int32, (2 * lanes, lanes), 1)
        for i in range(2):
            spread = (row == 2 * col + i).astype(f32).astype(bf16)
            for d in range(0, share, lanes):
                left[2 * d : 2 * (d + lanes), i * tokens : (i + 1) * tokens] = lax.dot_general(
                    spread,
                    held[:, d : d + lanes],
                    (((1,), (1,)), ((), ())),
                    preferred_element_type=f32,
                ).astype(bf16)

    return pl.pallas_call(
        kernel,
        in_specs=[anywhere] * blocks,
        out_specs=whole_vmem,
        out_shape=jax.ShapeDtypeStruct((2 * share, 2 * tokens), bf16),
        scratch_shapes=[
            pltpu.VMEM((tokens, share), bf16),
            pltpu.SemaphoreType.DMA((blocks,)),
        ],
        compiler_params=limits(20),
        name="spread_features",
    )(*in_hbm(*hiddens))


def head_pair(left, own, other, partner, so_far):
    tokens = left.shape[1] // 2
    share = left.shape[0] // 2
    piece = own.shape[2]
    cols = largest_tile(piece, 512, lanes)
    steps = piece // cols
    aliased = [] if so_far is None else [so_far]

    def kernel(left_ref, own_ref, other_ref, *refs):
        out_ref, ready, out_sem = refs[len(aliased) :]
        step = pl.program_id(0)
        slot = lax.rem(step, 2)
        base = 2 * (my_pair() ^ partner)

        def store(k, s):
            at = pl.ds(pl.multiple_of(k * cols, cols), cols)
            return pltpu.make_async_copy(
                ready.at[s], out_ref.at[:, 0, pl.ds(base, 2), at], out_sem.at[s]
            )

        @pl.when(step >= 2)
        def _():
            store(step - 2, slot).wait()

        right = jnp.concatenate([own_ref[0], other_ref[0], own_ref[1], other_ref[1]], axis=0)
        for d in range(0, 2 * share, 512):
            made = jnp.dot(left_ref[d : d + 512], right, preferred_element_type=f32).astype(bf16)
            ready[slot, d // 2 : d // 2 + 256] = made.reshape(256, 2, cols)
        store(step, slot).start()

        @pl.when(step == steps - 1)
        def _():
            if steps > 1:
                store(step - 1, 1 - slot).wait()
            store(step, slot).wait()

    return pl.pallas_call(
        kernel,
        grid=(steps,),
        in_specs=[whole_vmem]
        + [pl.BlockSpec((2, tokens // 2, cols), lambda r: (0, 0, r))] * 2
        + [anywhere] * len(aliased),
        out_specs=anywhere,
        out_shape=jax.ShapeDtypeStruct((share, 1, 4, piece), bf16),
        scratch_shapes=[
            pltpu.VMEM((2, share, 2, cols), bf16),
            pltpu.SemaphoreType.DMA((2,)),
        ],
        input_output_aliases={3: 0} if aliased else {},
        compiler_params=limits(20),
        cost_estimate=pl.CostEstimate(
            flops=8 * share * tokens * piece, bytes_accessed=4 * share * piece, transcendentals=0
        ),
        name="head_pair",
    )(left, *in_hbm(own, other), *aliased)


def on_device(hidden, head_weight, teacher):
    me_a = lax.axis_index("aa")
    me_b = lax.axis_index("ba")
    count = lax.axis_size("ba")
    near = count // 2
    few = teacher.shape[0]
    width = hidden.shape[1]
    tokens = few * count
    chip, core = me_a // 2, me_a % 2

    side = exchange(hidden, "aa", 2)
    beside = exchange(hidden, "aa", 1)
    *blocks, teacher_stat = split_teacher(teacher)
    blocks, beside, head_weight = lax.optimization_barrier((blocks, beside, head_weight))
    middle = near + (count - near) * 3 // 4
    teacher_stats = [teacher_stat, exchange(teacher_stat, "aa", 2)]
    arrived = [exchange(block, "ba", s) if s else block for s, block in enumerate(blocks[:near])]
    pair = take_pair(head_weight)
    arrived, teacher_stats, early, side, pair = lax.optimization_barrier(
        (arrived, teacher_stats, blocks[near:middle], side, pair)
    )
    hiddens = [hidden, beside, side, exchange(side, "aa", 1)]
    arrived += [exchange(block, "ba", near + s) for s, block in enumerate(early)]

    def cross(parts):
        mine = jnp.concatenate(parts, axis=0)
        return [mine, exchange(mine, "aa", 2)]

    def swap(group):
        return group + [exchange(part, "aa", 1) for part in group]

    group_a = cross(arrived[:near])
    first, stat_first = student_logits(hiddens, pair, 0)
    late, first, stat_first, pair = lax.optimization_barrier(
        (blocks[middle:], first, stat_first, pair)
    )
    arrived += [exchange(late[s - middle], "ba", s) for s in range(middle, count)]
    second, stat_second = student_logits(hiddens, pair, 1)
    arrived[near:middle], stat_second = lax.optimization_barrier((arrived[near:middle], stat_second))
    packed = pack_stats([stat_first, stat_second], teacher_stats)
    group_a, packed = lax.optimization_barrier((group_a, packed))
    group_a = swap(group_a)
    packed = merge_two(packed, exchange(packed, "aa", 1))
    group_b = cross(arrived[near:middle])
    mask = 1
    while 2 * mask < count:
        met = exchange(packed, "ba", mask)
        if mask == 1:
            left = spread_features(hiddens)
            left, met = lax.optimization_barrier((left, met))
        packed = merge_two(packed, met)
        if 4 * mask == count:
            last_parts, packed = lax.optimization_barrier((arrived[middle:], packed))
            group_c = cross(last_parts)
        mask *= 2
    met = exchange(packed, "ba", mask)
    group_b, group_c, met = lax.optimization_barrier((group_b, group_c, met))
    group_b, group_c = swap(group_b), swap(group_c)
    sums = all_log_sums(packed, met)
    groups = [group_a, group_b, group_c]

    def plan(group):
        is_far = (me_b // near) ^ group
        step = jnp.arange(near)
        place = (me_b % near) ^ step
        short = middle - near
        kind = jnp.where(is_far == 0, 0, jnp.where(step < short, 1, 2))
        reads = [
            jnp.where(is_far == 0, step, 0),
            jnp.where(is_far == 1, jnp.minimum(step, short - 1), 0),
            jnp.where(is_far == 1, jnp.maximum(step - short, 0), 0),
        ]
        return jnp.concatenate(
            [place, place + near * group, *reads, kind, core[None]]
        ).astype(jnp.int32)

    students = [first, second]
    grad_own, found = logit_gradient(plan(chip), groups, students, *sums)
    kept, sent = hidden_share(grad_own, pair)
    shares = share_out(kept, exchange(sent, "aa", 1), found)
    own_met = exchange(grad_own, "aa", 1)
    sums, own_met, shares = lax.optimization_barrier((sums, own_met, shares))
    grad_other, _ = logit_gradient(plan(1 - chip), groups, students, *sums)
    reduced = [exchange(shares[s], "ba", s) for s in range(1, count)]
    reduced, grad_other = lax.optimization_barrier((reduced, grad_other))
    summed = shares[0].astype(f32)
    for part in reduced:
        summed = summed + part.astype(f32)
    divergence = jnp.sum(summed[:, width:])[None] / tokens
    summed = summed[:, :width].astype(bf16)

    other_met = exchange(grad_other, "aa", 1)
    divergence = divergence + exchange(divergence, "aa", 1)
    gathered = {s: exchange(summed, "ba", s) for s in range(near - 1, count)}
    grad_own, summed = lax.optimization_barrier((grad_own, summed))
    grad_head = head_pair(left, grad_own, grad_other, 0, None)
    summed, gathered, grad_head, divergence, other_met = lax.optimization_barrier(
        (summed, gathered, grad_head, divergence, other_met)
    )
    for s in range(1, near - 1):
        gathered[s] = exchange(summed, "ba", s)
    divergence = divergence + exchange(divergence, "aa", 2)
    grad_head = head_pair(left, own_met, other_met, 1, grad_head)
    gathered, grad_head = lax.optimization_barrier((gathered, grad_head))
    grad_hidden = put_together([summed] + [gathered[s] for s in range(1, count)])
    return divergence[0], grad_hidden, grad_head


def solution(mesh):
    placed = (P("aa", None), P(None, "ba", None, None), P("ba", "aa", None, None))
    return jax.shard_map(
        on_device,
        mesh=mesh,
        in_specs=placed,
        out_specs=(P(), P("aa", None), P("aa", "ba", None, None)),
        check_vma=False,
    )
```

```python
import functools

import jax
import jax.numpy as jnp
from jax import lax
from jax.experimental import pallas as pl
from jax.experimental.pallas import tpu as pltpu
from jax.sharding import PartitionSpec as P

grad_scale = 256.0
lanes = 128
absent = -1e30
f32 = jnp.float32
bf16 = jnp.bfloat16
anywhere = pl.BlockSpec(memory_space=pl.ANY)
whole_vmem = pl.BlockSpec(memory_space=pltpu.VMEM)


def in_hbm(*values):
    return [pltpu.with_memory_space_constraint(value, pltpu.HBM) for value in values]


def in_vmem(value):
    return pltpu.with_memory_space_constraint(value, pltpu.VMEM)


def limits(mib):
    return pltpu.CompilerParams(vmem_limit_bytes=mib << 20)


def largest_tile(size, most, step):
    tile = min(size, most)
    while size % tile or tile % step:
        tile -= step
    return tile


def my_pair():
    me = lax.axis_index("aa")
    return (me % 2) ^ (me // 2)


def gate(values, deps):
    return lax.optimization_barrier((values, deps))[0]


def exchange(value, axis, mask):
    count = lax.axis_size(axis)
    return lax.ppermute(value, axis, [(i, i ^ mask) for i in range(count)])


def lane_row(column, rows):
    return jnp.transpose(jnp.broadcast_to(column, (rows, lanes)))[0:1]


def join(parts):
    starts = [sum(part.shape[0] for part in parts[:n]) for n in range(len(parts))]
    total = starts[-1] + parts[-1].shape[0]
    if any(part.shape[0] % 16 for part in parts):
        return jnp.concatenate(parts, axis=0)

    def kernel(*refs):
        given, (out_ref, sem) = refs[: len(parts)], refs[len(parts) :]
        copies = [
            pltpu.make_async_copy(ref, out_ref.at[pl.ds(start, ref.shape[0])], sem.at[n])
            for n, (ref, start) in enumerate(zip(given, starts))
        ]
        for copy in copies:
            copy.start()
        for copy in copies:
            copy.wait()

    return pl.pallas_call(
        kernel,
        in_specs=[anywhere] * len(parts),
        out_specs=anywhere,
        out_shape=pltpu.HBM((total, parts[0].shape[1]), bf16),
        scratch_shapes=[pltpu.SemaphoreType.DMA((len(parts),))],
        compiler_params=limits(4),
        name="join",
    )(*parts)


def split_teacher(teacher):
    tokens, _, owners, piece = teacher.shape
    every = tokens * owners
    cols = largest_tile(piece, 512, lanes)

    def kernel(in_ref, *refs):
        outs, (stat_ref, peak_ref, total_ref) = refs[:owners], refs[owners:]
        step = pl.program_id(0)
        me = lax.axis_index("ba")
        flat = in_ref[:, 0].reshape(every, cols)
        row = lax.broadcasted_iota(jnp.int32, (every, every), 0)
        col = lax.broadcasted_iota(jnp.int32, (every, every), 1)
        source = (row % tokens) * owners + ((row // tokens) ^ me)
        pick = (col == source).astype(f32).astype(bf16)
        moved = jnp.dot(pick, flat, preferred_element_type=f32)
        for s in range(owners):
            outs[s][...] = moved[s * tokens : (s + 1) * tokens].astype(bf16)
        parts = [
            moved[s * tokens : (s + 1) * tokens, k : k + lanes]
            for s in range(owners)
            for k in range(0, cols, lanes)
        ]
        peak = functools.reduce(jnp.maximum, parts)

        @pl.when(step == 0)
        def _():
            peak_ref[...] = peak
            total_ref[...] = jnp.zeros_like(total_ref)

        old = peak_ref[...]
        new = jnp.maximum(old, peak)
        total = total_ref[...] * jnp.exp(old - new)
        for part in parts:
            total = total + jnp.exp(part - new)
        peak_ref[...] = new
        total_ref[...] = total

        @pl.when(step == pl.num_programs(0) - 1)
        def _():
            top = jnp.max(new, axis=1, keepdims=True)
            summed = jnp.sum(total * jnp.exp(new - top), axis=1, keepdims=True)
            token = lax.broadcasted_iota(jnp.int32, (tokens, every), 0) + me * tokens
            here = token == lax.broadcasted_iota(jnp.int32, (tokens, every), 1)
            peaks = jnp.max(jnp.where(here, top, absent), axis=0, keepdims=True)
            sums = jnp.sum(jnp.where(here, summed, 0.0), axis=0, keepdims=True)
            stat_ref[0:1, :] = peaks
            stat_ref[1:2, :] = sums
            stat_ref[2:8, :] = jnp.zeros((6, every), f32)

    return pl.pallas_call(
        kernel,
        grid=(piece // cols,),
        in_specs=[pl.BlockSpec((tokens, 1, owners, cols), lambda r: (0, 0, 0, r))],
        out_specs=[pl.BlockSpec((tokens, cols), lambda r: (0, r))] * owners
        + [pl.BlockSpec((8, every), lambda r: (0, 0))],
        out_shape=[pltpu.HBM((tokens, piece), bf16)] * owners
        + [jax.ShapeDtypeStruct((8, every), f32)],
        scratch_shapes=[pltpu.VMEM((tokens, lanes), f32)] * 2,
        compiler_params=limits(20),
        name="split_teacher",
    )(*in_hbm(teacher))


def take_pair(head_weight):
    width, _, _, piece = head_weight.shape
    rows = largest_tile(width, 256, lanes)
    steps = width // rows
    depth = min(4, steps)

    def kernel(w_ref, out_ref, taken, in_sem):
        pair = my_pair()
        row = lax.broadcasted_iota(jnp.int32, (2 * lanes, 2 * lanes), 0)
        col = lax.broadcasted_iota(jnp.int32, (2 * lanes, 2 * lanes), 1)
        pick = (col == (row % lanes) * 2 + row // lanes).astype(f32).astype(bf16)

        def fetch(i):
            return pltpu.make_async_copy(
                w_ref.at[pl.ds(i * rows, rows), 0, pl.ds(2 * pair, 2), :],
                taken.at[i % depth],
                in_sem.at[i % depth],
            )

        for i in range(depth):
            fetch(i).start()
        for i in range(steps):
            fetch(i).wait()
            for q in range(0, rows, lanes):
                block = taken[i % depth, q : q + lanes].reshape(2 * lanes, piece)
                moved = jnp.dot(pick, block, preferred_element_type=f32).astype(bf16)
                at = i * rows + q
                out_ref[0, at : at + lanes] = moved[:lanes]
                out_ref[1, at : at + lanes] = moved[lanes:]
            if i + depth < steps:
                fetch(i + depth).start()

    return pl.pallas_call(
        kernel,
        in_specs=[anywhere],
        out_specs=whole_vmem,
        out_shape=pltpu.VMEM((2, width, piece), bf16),
        scratch_shapes=[
            pltpu.VMEM((depth, rows, 2, piece), bf16),
            pltpu.SemaphoreType.DMA((depth,)),
        ],
        compiler_params=limits(20),
        cost_estimate=pl.CostEstimate(
            flops=16 * lanes * width * piece,
            bytes_accessed=4 * width * piece,
            transcendentals=0,
        ),
        name="take_pair",
    )(head_weight)


def student_logits(hiddens, pair):
    rows, width = hiddens[0].shape
    blocks = len(hiddens)
    tokens = rows * blocks
    piece = pair.shape[2]
    cols = largest_tile(piece, 1024, lanes)
    part = largest_tile(cols, 256, lanes)

    def kernel(*refs):
        given, w_ref = refs[:blocks], refs[blocks]
        out_ref, stat_ref, left, peak_ref, total_ref, sem = refs[blocks + 1 :]
        first = (pl.program_id(0) == 0) & (pl.program_id(1) == 0)
        last = (pl.program_id(0) == 1) & (pl.program_id(1) == pl.num_programs(1) - 1)
        me = lax.axis_index("aa")

        @pl.when(first)
        def _():
            def place(q):
                at = pl.ds(pl.multiple_of((me ^ q) * rows, rows), rows)
                return pltpu.make_async_copy(given[q], left.at[at], sem.at[q])

            for q in range(blocks):
                place(q).start()
            peak_ref[...] = jnp.full_like(peak_ref, absent)
            total_ref[...] = jnp.zeros_like(total_ref)
            for q in range(blocks):
                place(q).wait()

        def collect(start):
            for k in range(0, tokens, 64):
                at = pl.ds(k, 64)
                parts = [out_ref[0, at, j : j + lanes] for j in range(start, start + part, lanes)]
                old = peak_ref[at]
                new = functools.reduce(jnp.maximum, parts, old)
                total = total_ref[at] * jnp.exp(old - new)
                for value in parts:
                    total = total + jnp.exp(value - new)
                peak_ref[at] = new
                total_ref[at] = total

        for n in range(0, cols, part):
            at = pl.ds(pl.multiple_of(pl.program_id(1) * cols + n, part), part)
            out_ref[0, :, n : n + part] = jnp.dot(
                left[...], w_ref[pl.program_id(0), :, at], preferred_element_type=f32
            )
            if n:
                collect(n - part)
        collect(cols - part)

        @pl.when(last)
        def _():
            peak = peak_ref[...]
            top = jnp.max(peak, axis=1, keepdims=True)
            summed = jnp.sum(total_ref[...] * jnp.exp(peak - top), axis=1, keepdims=True)
            stat_ref[0:1, :] = lane_row(top, tokens)
            stat_ref[1:2, :] = lane_row(summed, tokens)
            stat_ref[2:8, :] = jnp.zeros((6, tokens), f32)

    return pl.pallas_call(
        kernel,
        grid=(2, piece // cols),
        in_specs=[anywhere] * blocks
        + [whole_vmem],
        out_specs=[
            pl.BlockSpec((1, tokens, cols), lambda i, r: (i, 0, r)),
            pl.BlockSpec((8, tokens), lambda i, r: (0, 0)),
        ],
        out_shape=[
            pltpu.HBM((2, tokens, piece), f32),
            jax.ShapeDtypeStruct((8, tokens), f32),
        ],
        scratch_shapes=[
            pltpu.VMEM((tokens, width), bf16),
            pltpu.VMEM((tokens, lanes), f32),
            pltpu.VMEM((tokens, lanes), f32),
            pltpu.SemaphoreType.DMA((blocks,)),
        ],
        compiler_params=limits(20),
        cost_estimate=pl.CostEstimate(flops=1, bytes_accessed=1, transcendentals=0),
        name="student_logits",
    )(*in_hbm(*hiddens), in_vmem(pair))


def merge(stats, row=0):
    peak = functools.reduce(jnp.maximum, [s[row : row + 1] for s in stats])
    total = sum(s[row + 1 : row + 2] * jnp.exp(s[row : row + 1] - peak) for s in stats)
    return peak, total


def pack_stats(student_stats, teacher_stats):
    tokens = student_stats[0].shape[1]
    count = len(student_stats)

    def kernel(*refs):
        out_ref = refs[-1]
        peak, total = merge([r[...] for r in refs[:count]])
        out_ref[0:1, :] = peak
        out_ref[1:2, :] = total
        peak, total = merge([r[...] for r in refs[count:-1]])
        out_ref[2:3, :] = peak
        out_ref[3:4, :] = total
        out_ref[4:8, :] = jnp.zeros((4, tokens), f32)

    return pl.pallas_call(
        kernel,
        in_specs=[whole_vmem] * (count + len(teacher_stats)),
        out_specs=whole_vmem,
        out_shape=jax.ShapeDtypeStruct((8, tokens), f32),
        compiler_params=limits(20),
        name="pack_stats",
    )(*student_stats, *teacher_stats)


def merge_two(first, second):
    tokens = first.shape[1]

    def kernel(a_ref, b_ref, out_ref):
        both = [a_ref[...], b_ref[...]]
        for row in (0, 2):
            peak, total = merge(both, row)
            out_ref[row : row + 1, :] = peak
            out_ref[row + 1 : row + 2, :] = total
        out_ref[4:8, :] = jnp.zeros((4, tokens), f32)

    return pl.pallas_call(
        kernel,
        in_specs=[whole_vmem] * 2,
        out_specs=whole_vmem,
        out_shape=jax.ShapeDtypeStruct((8, tokens), f32),
        compiler_params=limits(20),
        name="merge_two",
    )(first, second)


def all_log_sums(first, second):
    tokens = first.shape[1]

    def kernel(a_ref, b_ref, *outs):
        both = [a_ref[...], b_ref[...]]
        for row, out_ref in zip((0, 2), outs):
            peak, total = merge(both, row)
            wide = jnp.broadcast_to(peak + jnp.log(total), (lanes, tokens))
            out_ref[...] = jnp.transpose(wide)

    return pl.pallas_call(
        kernel,
        in_specs=[whole_vmem] * 2,
        out_specs=[whole_vmem] * 2,
        out_shape=[pltpu.HBM((tokens, lanes), f32)] * 2,
        compiler_params=limits(20),
        name="all_log_sums",
    )(first, second)


def logit_gradient(plan, groups, student, student_sum, teacher_sum):
    count = (plan.shape[0] - 3) // 2
    _, tokens, piece = student.shape
    half = tokens // 2
    few = tokens // count
    per = 2 if count // 2 % 2 == 0 else 1
    steps = count // 2 // per
    cols = largest_tile(piece, 512, lanes)
    rows = 16

    def kernel(plan_ref, *refs):
        teachers = [refs[4 * n : 4 * n + 4] for n in range(len(groups))]
        s_ref, ssum_ref, tsum_ref, g_ref, div_ref, held, sem = refs[4 * len(groups) :]
        step = pl.program_id(0)
        slot = lax.rem(step, 2)
        core = plan_ref[2]

        def fetch(k, to):
            for m in range(per):
                s = (plan_ref[0] + k * per + m) ^ plan_ref[1]
                block = pl.ds(pl.multiple_of(plan_ref[3 + s] * few, few), few)
                for n, (own, side, own_met, side_met) in enumerate(teachers):
                    for at_core, ordered in enumerate(((own, own_met), (side_met, side))):

                        @pl.when((plan_ref[3 + count + s] == n) & (core == at_core))
                        def _(ordered=ordered, block=block, m=m):
                            for i in range(2):
                                pltpu.make_async_copy(
                                    ordered[i].at[block],
                                    held.at[to, i, pl.ds(m * few, few)],
                                    sem.at[to, i, m],
                                ).start()

        @pl.when(step == 0)
        def _():
            div_ref[...] = jnp.zeros_like(div_ref)
            fetch(0, 0)

        @pl.when(step + 1 < steps)
        def _():
            fetch(step + 1, 1 - slot)

        for i in range(2):
            for m in range(per):
                pltpu.make_async_copy(
                    teachers[0][0].at[pl.ds(0, few)],
                    held.at[slot, i, pl.ds(m * few, few)],
                    sem.at[slot, i, m],
                ).wait()

        @pl.loop(0, per * few // rows)
        def _(k):
            at = pl.ds(pl.multiple_of(k * rows, rows), rows)
            ssum = jnp.concatenate([ssum_ref[at]] * (cols // lanes), axis=1)
            tsum = jnp.concatenate([tsum_ref[at]] * (cols // lanes), axis=1)
            found = jnp.zeros((rows, cols), f32)
            for i in range(2):
                for j in range(0, piece, cols):
                    log_s = s_ref[i, at, j : j + cols] - ssum
                    log_t = held[slot, i, at, j : j + cols].astype(f32) - tsum
                    prob_t = jnp.exp(log_t)
                    g_ref[i, at, j : j + cols] = (
                        grad_scale * (jnp.exp(log_s) - prob_t)
                    ).astype(bf16)
                    found = found + prob_t * (log_t - log_s)
            folded = [
                found[m : m + 8, n : n + lanes]
                for m in range(0, rows, 8)
                for n in range(0, cols, lanes)
            ]
            div_ref[...] += sum(folded[1:], folded[0])

    return pl.pallas_call(
        kernel,
        grid_spec=pltpu.PrefetchScalarGridSpec(
            num_scalar_prefetch=1,
            grid=(steps,),
            in_specs=[anywhere] * (4 * len(groups))
            + [pl.BlockSpec((2, per * few, piece), lambda s, p: (0, p[0] // per + s, 0))]
            + [pl.BlockSpec((per * few, lanes), lambda s, p: (p[0] // per + s, 0))] * 2,
            out_specs=[
                pl.BlockSpec((2, per * few, piece), lambda s, p: (0, s, 0)),
                pl.BlockSpec((8, lanes), lambda s, p: (0, 0)),
            ],
            scratch_shapes=[
                pltpu.VMEM((2, 2, per * few, piece), bf16),
                pltpu.SemaphoreType.DMA((2, 2, per)),
            ],
        ),
        out_shape=[
            pltpu.HBM((2, half, piece), bf16),
            jax.ShapeDtypeStruct((8, lanes), f32),
        ],
        compiler_params=limits(20),
        cost_estimate=pl.CostEstimate(
            flops=8 * half * piece, bytes_accessed=16 * half * piece, transcendentals=4 * half * piece
        ),
        name="logit_gradient",
    )(
        plan,
        *in_hbm(*[part for group in groups for part in group]),
        *in_hbm(student, student_sum, teacher_sum),
    )


def hidden_share(gradient, pair):
    _, tokens, piece = gradient.shape
    width = pair.shape[1]
    half = tokens // 2
    cols = largest_tile(width, 512, lanes)
    steps = width // cols
    depth = min(3, steps)

    def kernel(given_ref, w_ref, kept_ref, sent_ref, g_ref, taken, sem):
        core = lax.axis_index("aa") % 2

        def fetch(k):
            at = pl.ds(k * cols, cols)
            return pltpu.make_async_copy(w_ref.at[:, at, :], taken.at[k % depth], sem.at[k % depth])

        load = pltpu.make_async_copy(given_ref, g_ref, sem.at[depth])
        load.start()
        for k in range(depth):
            fetch(k).start()
        load.wait()
        for k in range(steps):
            fetch(k).wait()
            total = sum(
                lax.dot_general(
                    g_ref[i],
                    taken[k % depth, i],
                    (((1,), (1,)), ((), ())),
                    preferred_element_type=f32,
                )
                for i in range(2)
            )
            if k + depth < steps:
                fetch(k + depth).start()
            at = slice(k * cols, (k + 1) * cols)

            @pl.when(core == 0)
            def _(total=total, at=at):
                kept_ref[:, at] = total[:half]
                sent_ref[:, at] = total[half:].astype(bf16)

            @pl.when(core == 1)
            def _(total=total, at=at):
                kept_ref[:, at] = total[half:]
                sent_ref[:, at] = total[:half].astype(bf16)

    return pl.pallas_call(
        kernel,
        in_specs=[anywhere] * 2,
        out_specs=[whole_vmem] * 2,
        out_shape=[
            pltpu.VMEM((half, width), f32),
            pltpu.VMEM((half, width), bf16),
        ],
        scratch_shapes=[
            pltpu.VMEM((2, tokens, piece), bf16),
            pltpu.VMEM((depth, 2, cols, piece), bf16),
            pltpu.SemaphoreType.DMA((depth + 1,)),
        ],
        compiler_params=limits(24),
        cost_estimate=pl.CostEstimate(
            flops=4 * tokens * width * piece, bytes_accessed=4 * width * piece, transcendentals=0
        ),
        name="hidden_share",
    )(*in_hbm(gradient, pair))


def three_parts(value):
    high = lax.reduce_precision(value, 8, 7)
    rest = value - high
    middle = lax.reduce_precision(rest, 8, 7)
    return high, middle, rest - middle


def share_out(kept, arrived, found):
    rows, width = kept.shape
    count = lax.axis_size("ba")
    few = rows // count
    if few % 16:
        order = lax.axis_index("ba") ^ jnp.arange(count)
        summed = (kept + arrived.astype(f32)).astype(bf16).reshape(count, few, width)
        parts = jnp.stack(three_parts(jnp.sum(found))).astype(bf16)
        carried = jnp.zeros((few, lanes), bf16).at[0, :3].set(parts)
        return [jnp.concatenate([summed[order[s]], carried], axis=1) for s in range(count)]

    def kernel(kept_ref, arrived_ref, found_ref, *outs):
        me = lax.axis_index("ba")
        total = jnp.sum(found_ref[...], axis=0, keepdims=True)
        total = jnp.sum(total, axis=1, keepdims=True)
        high = total.astype(bf16).astype(f32)
        middle = (total - high).astype(bf16).astype(f32)
        low = total - high - middle
        lane = lax.broadcasted_iota(jnp.int32, (few, lanes), 1)
        lane = lane + lanes * lax.broadcasted_iota(jnp.int32, (few, lanes), 0)
        carried = jnp.where(lane == 0, high, jnp.where(lane == 1, middle, jnp.where(lane == 2, low, 0.0)))
        for s in range(count):
            at = pl.ds(pl.multiple_of((me ^ s) * few, few), few)
            outs[s][:, :width] = (kept_ref[at] + arrived_ref[at].astype(f32)).astype(bf16)
            outs[s][:, width:] = carried.astype(bf16)

    return pl.pallas_call(
        kernel,
        in_specs=[whole_vmem] * 3,
        out_specs=[whole_vmem] * count,
        out_shape=[jax.ShapeDtypeStruct((few, width + lanes), bf16)] * count,
        compiler_params=limits(20),
        name="share_out",
    )(in_vmem(kept), in_vmem(arrived), found)


def put_together(even, odd, few):
    rows, width = even.shape
    count = rows // few
    if few % 16:
        mine = lax.axis_index("ba") ^ jnp.arange(2 * count)
        both = jnp.stack([even.reshape(count, few, width), odd.reshape(count, few, width)], axis=1)
        return both.reshape(2 * count, few, width)[mine].reshape(2 * rows, width)

    def kernel(even_ref, odd_ref, out_ref, sem):
        me = lax.axis_index("ba")

        def place(s):
            to = pl.ds(pl.multiple_of((me ^ s) * few, few), few)
            ref = (even_ref, odd_ref)[s % 2]
            return pltpu.make_async_copy(ref.at[pl.ds(s // 2 * few, few)], out_ref.at[to], sem.at[s])

        for s in range(2 * count):
            place(s).start()
        for s in range(2 * count):
            place(s).wait()

    return pl.pallas_call(
        kernel,
        in_specs=[anywhere] * 2,
        out_specs=anywhere,
        out_shape=pltpu.HBM((2 * rows, width), bf16),
        scratch_shapes=[pltpu.SemaphoreType.DMA((2 * count,))],
        compiler_params=limits(4),
        name="put_together",
    )(even, odd)


def turn_features(hiddens):
    rows, width = hiddens[0].shape
    blocks = len(hiddens)
    tokens = rows * blocks
    share = width // blocks

    def kernel(*refs):
        given = refs[:blocks]
        left, held, sem = refs[blocks:]
        me = lax.axis_index("aa")

        def place(q):
            block = q // 2 * 2 + ((me % 2) ^ (q % 2))
            at = pl.ds(pl.multiple_of(block * rows, rows), rows)
            part = pl.ds(pl.multiple_of(me * share, share), share)
            return pltpu.make_async_copy(given[q].at[:, part], held.at[at], sem.at[q])

        for q in range(blocks):
            place(q).start()
        for q in range(blocks):
            place(q).wait()
        row = lax.broadcasted_iota(jnp.int32, (lanes, lanes), 0)
        col = lax.broadcasted_iota(jnp.int32, (lanes, lanes), 1)
        same = (row == col).astype(f32).astype(bf16)
        for d in range(0, share, lanes):
            left[d : d + lanes] = lax.dot_general(
                same, held[:, d : d + lanes], (((1,), (1,)), ((), ())), preferred_element_type=f32
            ).astype(bf16)

    return pl.pallas_call(
        kernel,
        in_specs=[anywhere] * blocks,
        out_specs=whole_vmem,
        out_shape=jax.ShapeDtypeStruct((share, tokens), bf16),
        scratch_shapes=[
            pltpu.VMEM((tokens, share), bf16),
            pltpu.SemaphoreType.DMA((blocks,)),
        ],
        compiler_params=limits(20),
        name="turn_features",
    )(*in_hbm(*hiddens))


def head_pair(left, own, other, partner, so_far):
    share, tokens = left.shape
    piece = own.shape[2]
    cols = largest_tile(piece, 512, lanes)
    part = largest_tile(cols, 256, lanes)
    steps = piece // cols
    aliased = [] if so_far is None else [so_far]

    def kernel(left_ref, own_ref, other_ref, *refs):
        out_ref, mixed, ready, out_sem = refs[len(aliased) :]
        step = pl.program_id(0)
        slot = lax.rem(step, 2)
        base = 2 * (my_pair() ^ partner)

        def store(k, s):
            at = pl.ds(pl.multiple_of(k * cols, cols), cols)
            return pltpu.make_async_copy(
                ready.at[s], out_ref.at[:, 0, pl.ds(base, 2), at], out_sem.at[s]
            )

        @pl.when(step >= 2)
        def _():
            store(step - 2, slot).wait()

        def unload(start):
            for n in range(start // lanes, (start + part) // lanes):
                ready[slot, :, :, n * lanes : (n + 1) * lanes] = (
                    mixed[n].astype(bf16).reshape(share, 2, lanes)
                )

        for j in range(0, cols, part):
            for i in range(2):
                right = jnp.concatenate(
                    [own_ref[i, :, j : j + part], other_ref[i, :, j : j + part]], axis=0
                )
                made = jnp.dot(left_ref[...], right, preferred_element_type=f32)
                for n in range(part // lanes):
                    mixed[j // lanes + n, pl.ds(i, share, stride=2), :] = made[
                        :, n * lanes : (n + 1) * lanes
                    ]
            if j:
                unload(j - part)
        unload(cols - part)
        store(step, slot).start()

        @pl.when(step == steps - 1)
        def _():
            if steps > 1:
                store(step - 1, 1 - slot).wait()
            store(step, slot).wait()

    return pl.pallas_call(
        kernel,
        grid=(steps,),
        in_specs=[whole_vmem]
        + [pl.BlockSpec((2, tokens // 2, cols), lambda r: (0, 0, r))] * 2
        + [anywhere] * len(aliased),
        out_specs=anywhere,
        out_shape=jax.ShapeDtypeStruct((share, 1, 4, piece), bf16),
        scratch_shapes=[
            pltpu.VMEM((cols // lanes, 2 * share, lanes), f32),
            pltpu.VMEM((2, share, 2, cols), bf16),
            pltpu.SemaphoreType.DMA((2,)),
        ],
        input_output_aliases={3: 0} if aliased else {},
        compiler_params=limits(30),
        cost_estimate=pl.CostEstimate(
            flops=4 * share * tokens * piece, bytes_accessed=4 * share * piece, transcendentals=0
        ),
        name="head_pair",
    )(left, *in_hbm(own, other), *aliased)


def on_device(hidden, head_weight, teacher):
    me_a = lax.axis_index("aa")
    me_b = lax.axis_index("ba")
    count = lax.axis_size("ba")
    near = count // 2
    few = teacher.shape[0]
    width = hidden.shape[1]
    tokens = few * count
    chip, core = me_a // 2, me_a % 2

    side = exchange(hidden, "aa", 2)
    beside = exchange(hidden, "aa", 1)
    *blocks, teacher_stat = split_teacher(teacher)
    blocks, beside, head_weight = lax.optimization_barrier((blocks, beside, head_weight))
    middle = near + 1
    queue = [*range(near - 1), near, near + 1, near - 1, *range(near + 2, count)]
    arrived = [exchange(blocks[s], "ba", s) if s else blocks[s] for s in queue[:middle]]
    pair = take_pair(head_weight)
    teacher_stat, late, side, pair = lax.optimization_barrier(
        (teacher_stat, [blocks[s] for s in queue[middle:]], side, pair)
    )
    hiddens = [hidden, beside, side, exchange(side, "aa", 1)]
    arrived += [exchange(block, "ba", s) for block, s in zip(late, queue[middle:])]
    teacher_stats = [teacher_stat, exchange(teacher_stat, "aa", 2)]
    arrived[:middle], pair = lax.optimization_barrier((arrived[:middle], pair))

    def cross(parts):
        mine = join(parts)
        return [mine, exchange(mine, "aa", 2)]

    def swap(group):
        return group + [exchange(part, "aa", 1) for part in group]

    group_a = cross(arrived[:middle])
    student, student_stat = student_logits(hiddens, pair)
    arrived[middle:], student_stat = lax.optimization_barrier((arrived[middle:], student_stat))
    packed = pack_stats([student_stat], teacher_stats)
    group_a, packed = lax.optimization_barrier((group_a, packed))
    group_a = swap(group_a)
    group_b = cross(arrived[middle:])
    packed = merge_two(packed, exchange(packed, "aa", 1))
    mask = 1
    while 2 * mask < count:
        met = exchange(packed, "ba", mask)
        if mask == 1:
            left = turn_features(hiddens)
            left, met = lax.optimization_barrier((left, met))
        packed = merge_two(packed, met)
        mask *= 2
    group_a, packed = lax.optimization_barrier((group_a, packed))
    sums = all_log_sums(packed, exchange(packed, "ba", mask))
    group_b, sums = lax.optimization_barrier((group_b, sums))
    groups = [group_a, swap(group_b)]

    order = [queue.index(s) for s in range(count)]
    table = [n % middle if n < middle else n - middle for n in order] + [int(n >= middle) for n in order]

    def plan(group):
        here = jnp.stack([near * group, me_b, core]).astype(jnp.int32)
        return jnp.concatenate([here, jnp.array(table, jnp.int32)])

    grad_own, found = logit_gradient(plan(chip), groups, student, *sums)
    kept, sent = hidden_share(grad_own, pair)
    shares = share_out(kept, exchange(sent, "aa", 1), found)
    own_met = exchange(grad_own, "aa", 1)
    sums, own_met, shares = lax.optimization_barrier((sums, own_met, shares))
    grad_other, _ = logit_gradient(plan(1 - chip), groups, student, *sums)
    reduced = [exchange(shares[s], "ba", s) for s in range(1, count)]
    reduced, grad_other = lax.optimization_barrier((reduced, grad_other))
    summed = shares[0].astype(f32)
    for part in reduced:
        summed = summed + part.astype(f32)
    divergence = jnp.sum(summed[:, width:])[None] / tokens
    summed = summed[:, :width].astype(bf16)

    other_met = exchange(grad_other, "aa", 1)
    divergence = divergence + exchange(divergence, "aa", 1)
    gathered = [summed] + [exchange(summed, "ba", s) for s in range(2, count, 2)]
    grad_own, gathered[0] = lax.optimization_barrier((grad_own, gathered[0]))
    grad_head = head_pair(left, grad_own, grad_other, 0, None)
    gathered, grad_head, divergence, other_met = lax.optimization_barrier(
        (gathered, grad_head, divergence, other_met)
    )
    even = join(gathered)
    odd = exchange(even, "ba", 1)
    divergence = divergence + exchange(divergence, "aa", 2)
    even, other_met = lax.optimization_barrier((even, other_met))
    grad_head = head_pair(left, own_met, other_met, 1, grad_head)
    odd, grad_head = lax.optimization_barrier((odd, grad_head))
    grad_hidden = put_together(even, odd, summed.shape[0])
    return divergence[0], grad_hidden, grad_head


def solution(mesh):
    placed = (P("aa", None), P(None, "ba", None, None), P("ba", "aa", None, None))
    return jax.shard_map(
        on_device,
        mesh=mesh,
        in_specs=placed,
        out_specs=(P(), P("aa", None), P("aa", "ba", None, None)),
        check_vma=False,
    )
```

```python
import functools

import jax
import jax.numpy as jnp
from jax import lax
from jax.experimental import pallas as pl
from jax.experimental.pallas import tpu as pltpu
from jax.sharding import PartitionSpec as P

grad_scale = 256.0
lanes = 128
absent = -1e30
f32 = jnp.float32
bf16 = jnp.bfloat16
anywhere = pl.BlockSpec(memory_space=pl.ANY)
whole_vmem = pl.BlockSpec(memory_space=pltpu.VMEM)


def in_hbm(*values):
    return [pltpu.with_memory_space_constraint(value, pltpu.HBM) for value in values]


def in_vmem(value):
    return pltpu.with_memory_space_constraint(value, pltpu.VMEM)


def limits(mib):
    return pltpu.CompilerParams(vmem_limit_bytes=mib << 20)


def largest_tile(size, most, step):
    tile = min(size, most)
    while size % tile or tile % step:
        tile -= step
    return tile


def my_pair():
    me = lax.axis_index("aa")
    return (me % 2) ^ (me // 2)


def gate(values, deps):
    return lax.optimization_barrier((values, deps))[0]


def exchange(value, axis, mask):
    count = lax.axis_size(axis)
    return lax.ppermute(value, axis, [(i, i ^ mask) for i in range(count)])


def lane_row(column, rows):
    return jnp.transpose(jnp.broadcast_to(column, (rows, lanes)))[0:1]


def join(parts):
    starts = [sum(part.shape[0] for part in parts[:n]) for n in range(len(parts))]
    total = starts[-1] + parts[-1].shape[0]
    if len(parts) == 1:
        return parts[0]
    if any(part.shape[0] % 16 for part in parts):
        return jnp.concatenate(parts, axis=0)

    def kernel(*refs):
        given, (out_ref, sem) = refs[: len(parts)], refs[len(parts) :]
        copies = [
            pltpu.make_async_copy(ref, out_ref.at[pl.ds(start, ref.shape[0])], sem.at[n])
            for n, (ref, start) in enumerate(zip(given, starts))
        ]
        for copy in copies:
            copy.start()
        for copy in copies:
            copy.wait()

    return pl.pallas_call(
        kernel,
        in_specs=[anywhere] * len(parts),
        out_specs=anywhere,
        out_shape=pltpu.HBM((total, parts[0].shape[1]), bf16),
        scratch_shapes=[pltpu.SemaphoreType.DMA((len(parts),))],
        compiler_params=limits(4),
        name="join",
    )(*parts)


def split_teacher(teacher):
    tokens, _, owners, piece = teacher.shape
    every = tokens * owners
    cols = largest_tile(piece, 1024, lanes)

    def kernel(in_ref, *refs):
        outs, (stat_ref, peak_ref, total_ref) = refs[:owners], refs[owners:]
        step = pl.program_id(0)
        me = lax.axis_index("ba")
        flat = in_ref[:, 0].reshape(every, cols)
        row = lax.broadcasted_iota(jnp.int32, (every, every), 0)
        col = lax.broadcasted_iota(jnp.int32, (every, every), 1)
        source = (row % tokens) * owners + ((row // tokens) ^ me)
        pick = (col == source).astype(f32).astype(bf16)
        moved = jnp.dot(pick, flat, preferred_element_type=f32)
        for s in range(owners):
            outs[s][...] = moved[s * tokens : (s + 1) * tokens].astype(bf16)
        parts = [
            moved[s * tokens : (s + 1) * tokens, k : k + lanes]
            for s in range(owners)
            for k in range(0, cols, lanes)
        ]
        peak = functools.reduce(jnp.maximum, parts)

        @pl.when(step == 0)
        def _():
            peak_ref[...] = peak
            total_ref[...] = jnp.zeros_like(total_ref)

        old = peak_ref[...]
        new = jnp.maximum(old, peak)
        total = total_ref[...] * jnp.exp(old - new)
        for part in parts:
            total = total + jnp.exp(part - new)
        peak_ref[...] = new
        total_ref[...] = total

        @pl.when(step == pl.num_programs(0) - 1)
        def _():
            top = jnp.max(new, axis=1, keepdims=True)
            summed = jnp.sum(total * jnp.exp(new - top), axis=1, keepdims=True)
            token = lax.broadcasted_iota(jnp.int32, (tokens, every), 0) + me * tokens
            here = token == lax.broadcasted_iota(jnp.int32, (tokens, every), 1)
            peaks = jnp.max(jnp.where(here, top, absent), axis=0, keepdims=True)
            sums = jnp.sum(jnp.where(here, summed, 0.0), axis=0, keepdims=True)
            stat_ref[0:1, :] = peaks
            stat_ref[1:2, :] = sums
            stat_ref[2:8, :] = jnp.zeros((6, every), f32)

    return pl.pallas_call(
        kernel,
        grid=(piece // cols,),
        in_specs=[pl.BlockSpec((tokens, 1, owners, cols), lambda r: (0, 0, 0, r))],
        out_specs=[pl.BlockSpec((tokens, cols), lambda r: (0, r))] * owners
        + [pl.BlockSpec((8, every), lambda r: (0, 0))],
        out_shape=[pltpu.HBM((tokens, piece), bf16)] * owners
        + [jax.ShapeDtypeStruct((8, every), f32)],
        scratch_shapes=[pltpu.VMEM((tokens, lanes), f32)] * 2,
        compiler_params=limits(20),
        name="split_teacher",
    )(*in_hbm(teacher))


def take_pair(head_weight):
    width, _, _, piece = head_weight.shape
    rows = largest_tile(width, 256, lanes)
    steps = width // rows
    depth = min(4, steps)

    def kernel(w_ref, out_ref, taken, in_sem):
        pair = my_pair()
        row = lax.broadcasted_iota(jnp.int32, (2 * lanes, 2 * lanes), 0)
        col = lax.broadcasted_iota(jnp.int32, (2 * lanes, 2 * lanes), 1)
        pick = (col == (row % lanes) * 2 + row // lanes).astype(f32).astype(bf16)

        def fetch(i):
            return pltpu.make_async_copy(
                w_ref.at[pl.ds(i * rows, rows), 0, pl.ds(2 * pair, 2), :],
                taken.at[i % depth],
                in_sem.at[i % depth],
            )

        for i in range(depth):
            fetch(i).start()
        for i in range(steps):
            fetch(i).wait()
            for q in range(0, rows, lanes):
                block = taken[i % depth, q : q + lanes].reshape(2 * lanes, piece)
                moved = jnp.dot(pick, block, preferred_element_type=f32).astype(bf16)
                at = i * rows + q
                out_ref[0, at : at + lanes] = moved[:lanes]
                out_ref[1, at : at + lanes] = moved[lanes:]
            if i + depth < steps:
                fetch(i + depth).start()

    return pl.pallas_call(
        kernel,
        in_specs=[anywhere],
        out_specs=whole_vmem,
        out_shape=pltpu.VMEM((2, width, piece), bf16),
        scratch_shapes=[
            pltpu.VMEM((depth, rows, 2, piece), bf16),
            pltpu.SemaphoreType.DMA((depth,)),
        ],
        compiler_params=limits(20),
        cost_estimate=pl.CostEstimate(
            flops=16 * lanes * width * piece,
            bytes_accessed=4 * width * piece,
            transcendentals=0,
        ),
        name="take_pair",
    )(head_weight)


def student_logits(hiddens, pair):
    rows, width = hiddens[0].shape
    blocks = len(hiddens)
    tokens = rows * blocks
    piece = pair.shape[2]
    cols = largest_tile(piece, 1024, lanes)
    part = largest_tile(cols, 256, lanes)

    def kernel(*refs):
        given, w_ref = refs[:blocks], refs[blocks]
        out_ref, stat_ref, left, peak_ref, total_ref, sem = refs[blocks + 1 :]
        first = (pl.program_id(0) == 0) & (pl.program_id(1) == 0)
        last = (pl.program_id(0) == 1) & (pl.program_id(1) == pl.num_programs(1) - 1)
        me = lax.axis_index("aa")

        @pl.when(first)
        def _():
            def place(q):
                at = pl.ds(pl.multiple_of((me ^ q) * rows, rows), rows)
                return pltpu.make_async_copy(given[q], left.at[at], sem.at[q])

            for q in range(blocks):
                place(q).start()
            peak_ref[...] = jnp.full_like(peak_ref, absent)
            total_ref[...] = jnp.zeros_like(total_ref)
            for q in range(blocks):
                place(q).wait()

        def collect(start):
            for k in range(0, tokens, 64):
                at = pl.ds(k, 64)
                parts = [out_ref[0, at, j : j + lanes] for j in range(start, start + part, lanes)]
                old = peak_ref[at]
                new = functools.reduce(jnp.maximum, parts, old)
                total = total_ref[at] * jnp.exp(old - new)
                for value in parts:
                    total = total + jnp.exp(value - new)
                peak_ref[at] = new
                total_ref[at] = total

        for n in range(0, cols, part):
            at = pl.ds(pl.multiple_of(pl.program_id(1) * cols + n, part), part)
            out_ref[0, :, n : n + part] = jnp.dot(
                left[...], w_ref[pl.program_id(0), :, at], preferred_element_type=f32
            )
            if n:
                collect(n - part)
        collect(cols - part)

        @pl.when(last)
        def _():
            peak = peak_ref[...]
            top = jnp.max(peak, axis=1, keepdims=True)
            summed = jnp.sum(total_ref[...] * jnp.exp(peak - top), axis=1, keepdims=True)
            stat_ref[0:1, :] = lane_row(top, tokens)
            stat_ref[1:2, :] = lane_row(summed, tokens)
            stat_ref[2:8, :] = jnp.zeros((6, tokens), f32)

    return pl.pallas_call(
        kernel,
        grid=(2, piece // cols),
        in_specs=[anywhere] * blocks
        + [whole_vmem],
        out_specs=[
            pl.BlockSpec((1, tokens, cols), lambda i, r: (i, 0, r)),
            pl.BlockSpec((8, tokens), lambda i, r: (0, 0)),
        ],
        out_shape=[
            pltpu.HBM((2, tokens, piece), f32),
            jax.ShapeDtypeStruct((8, tokens), f32),
        ],
        scratch_shapes=[
            pltpu.VMEM((tokens, width), bf16),
            pltpu.VMEM((tokens, lanes), f32),
            pltpu.VMEM((tokens, lanes), f32),
            pltpu.SemaphoreType.DMA((blocks,)),
        ],
        compiler_params=limits(20),
        cost_estimate=pl.CostEstimate(flops=1, bytes_accessed=1, transcendentals=0),
        name="student_logits",
    )(*in_hbm(*hiddens), in_vmem(pair))


def merge(stats, row=0):
    peak = functools.reduce(jnp.maximum, [s[row : row + 1] for s in stats])
    total = sum(s[row + 1 : row + 2] * jnp.exp(s[row : row + 1] - peak) for s in stats)
    return peak, total


def pack_stats(student_stats, teacher_stats):
    tokens = student_stats[0].shape[1]
    count = len(student_stats)

    def kernel(*refs):
        out_ref = refs[-1]
        peak, total = merge([r[...] for r in refs[:count]])
        out_ref[0:1, :] = peak
        out_ref[1:2, :] = total
        peak, total = merge([r[...] for r in refs[count:-1]])
        out_ref[2:3, :] = peak
        out_ref[3:4, :] = total
        out_ref[4:8, :] = jnp.zeros((4, tokens), f32)

    return pl.pallas_call(
        kernel,
        in_specs=[whole_vmem] * (count + len(teacher_stats)),
        out_specs=whole_vmem,
        out_shape=jax.ShapeDtypeStruct((8, tokens), f32),
        compiler_params=limits(20),
        name="pack_stats",
    )(*student_stats, *teacher_stats)


def merge_two(first, second):
    tokens = first.shape[1]

    def kernel(a_ref, b_ref, out_ref):
        both = [a_ref[...], b_ref[...]]
        for row in (0, 2):
            peak, total = merge(both, row)
            out_ref[row : row + 1, :] = peak
            out_ref[row + 1 : row + 2, :] = total
        out_ref[4:8, :] = jnp.zeros((4, tokens), f32)

    return pl.pallas_call(
        kernel,
        in_specs=[whole_vmem] * 2,
        out_specs=whole_vmem,
        out_shape=jax.ShapeDtypeStruct((8, tokens), f32),
        compiler_params=limits(20),
        name="merge_two",
    )(first, second)


def all_log_sums(first, second):
    tokens = first.shape[1]

    def kernel(a_ref, b_ref, *outs):
        both = [a_ref[...], b_ref[...]]
        for row, out_ref in zip((0, 2), outs):
            peak, total = merge(both, row)
            wide = jnp.broadcast_to(peak + jnp.log(total), (lanes, tokens))
            out_ref[...] = jnp.transpose(wide)

    return pl.pallas_call(
        kernel,
        in_specs=[whole_vmem] * 2,
        out_specs=[whole_vmem] * 2,
        out_shape=[pltpu.HBM((tokens, lanes), f32)] * 2,
        compiler_params=limits(20),
        name="all_log_sums",
    )(first, second)


def logit_gradient(plan, groups, student, student_sum, teacher_sum):
    count = (plan.shape[0] - 3) // 2
    _, tokens, piece = student.shape
    half = tokens // 2
    few = tokens // count
    per = 2 if count // 2 % 2 == 0 else 1
    steps = count // 2 // per
    cols = largest_tile(piece, 512, lanes)
    rows = 16

    def kernel(plan_ref, *refs):
        teachers = [refs[4 * n : 4 * n + 4] for n in range(len(groups))]
        s_ref, ssum_ref, tsum_ref, g_ref, div_ref, held, sem = refs[4 * len(groups) :]
        step = pl.program_id(0)
        slot = lax.rem(step, 2)
        core = plan_ref[2]

        def fetch(k, to):
            for m in range(per):
                s = (plan_ref[0] + k * per + m) ^ plan_ref[1]
                block = pl.ds(pl.multiple_of(plan_ref[3 + s] * few, few), few)
                for n, (own, side, own_met, side_met) in enumerate(teachers):
                    for at_core, ordered in enumerate(((own, own_met), (side_met, side))):

                        @pl.when((plan_ref[3 + count + s] == n) & (core == at_core))
                        def _(ordered=ordered, block=block, m=m):
                            for i in range(2):
                                pltpu.make_async_copy(
                                    ordered[i].at[block],
                                    held.at[to, i, pl.ds(m * few, few)],
                                    sem.at[to, i, m],
                                ).start()

        @pl.when(step == 0)
        def _():
            div_ref[...] = jnp.zeros_like(div_ref)
            fetch(0, 0)

        @pl.when(step + 1 < steps)
        def _():
            fetch(step + 1, 1 - slot)

        for i in range(2):
            for m in range(per):
                pltpu.make_async_copy(
                    teachers[0][0].at[pl.ds(0, few)],
                    held.at[slot, i, pl.ds(m * few, few)],
                    sem.at[slot, i, m],
                ).wait()

        @pl.loop(0, per * few // rows)
        def _(k):
            at = pl.ds(pl.multiple_of(k * rows, rows), rows)
            ssum = jnp.concatenate([ssum_ref[at]] * (cols // lanes), axis=1)
            tsum = jnp.concatenate([tsum_ref[at]] * (cols // lanes), axis=1)
            found = jnp.zeros((rows, cols), f32)
            for i in range(2):
                for j in range(0, piece, cols):
                    log_s = s_ref[i, at, j : j + cols] - ssum
                    log_t = held[slot, i, at, j : j + cols].astype(f32) - tsum
                    prob_t = jnp.exp(log_t)
                    g_ref[i, at, j : j + cols] = (
                        grad_scale * (jnp.exp(log_s) - prob_t)
                    ).astype(bf16)
                    found = found + prob_t * (log_t - log_s)
            folded = [
                found[m : m + 8, n : n + lanes]
                for m in range(0, rows, 8)
                for n in range(0, cols, lanes)
            ]
            div_ref[...] += sum(folded[1:], folded[0])

    return pl.pallas_call(
        kernel,
        grid_spec=pltpu.PrefetchScalarGridSpec(
            num_scalar_prefetch=1,
            grid=(steps,),
            in_specs=[anywhere] * (4 * len(groups))
            + [pl.BlockSpec((2, per * few, piece), lambda s, p: (0, p[0] // per + s, 0))]
            + [pl.BlockSpec((per * few, lanes), lambda s, p: (p[0] // per + s, 0))] * 2,
            out_specs=[
                pl.BlockSpec((2, per * few, piece), lambda s, p: (0, s, 0)),
                pl.BlockSpec((8, lanes), lambda s, p: (0, 0)),
            ],
            scratch_shapes=[
                pltpu.VMEM((2, 2, per * few, piece), bf16),
                pltpu.SemaphoreType.DMA((2, 2, per)),
            ],
        ),
        out_shape=[
            pltpu.HBM((2, half, piece), bf16),
            jax.ShapeDtypeStruct((8, lanes), f32),
        ],
        compiler_params=limits(20),
        cost_estimate=pl.CostEstimate(
            flops=8 * half * piece, bytes_accessed=16 * half * piece, transcendentals=4 * half * piece
        ),
        name="logit_gradient",
    )(
        plan,
        *in_hbm(*[part for group in groups for part in group]),
        *in_hbm(student, student_sum, teacher_sum),
    )


def hidden_share(gradient, pair):
    _, tokens, piece = gradient.shape
    width = pair.shape[1]
    half = tokens // 2
    cols = largest_tile(width, 512, lanes)
    steps = width // cols
    depth = min(3, steps)

    def kernel(given_ref, w_ref, kept_ref, sent_ref, g_ref, taken, sem):
        core = lax.axis_index("aa") % 2

        def fetch(k):
            at = pl.ds(k * cols, cols)
            return pltpu.make_async_copy(w_ref.at[:, at, :], taken.at[k % depth], sem.at[k % depth])

        load = pltpu.make_async_copy(given_ref, g_ref, sem.at[depth])
        load.start()
        for k in range(depth):
            fetch(k).start()
        load.wait()
        for k in range(steps):
            fetch(k).wait()
            total = sum(
                lax.dot_general(
                    g_ref[i],
                    taken[k % depth, i],
                    (((1,), (1,)), ((), ())),
                    preferred_element_type=f32,
                )
                for i in range(2)
            )
            if k + depth < steps:
                fetch(k + depth).start()
            at = slice(k * cols, (k + 1) * cols)

            @pl.when(core == 0)
            def _(total=total, at=at):
                kept_ref[:, at] = total[:half]
                sent_ref[:, at] = total[half:].astype(bf16)

            @pl.when(core == 1)
            def _(total=total, at=at):
                kept_ref[:, at] = total[half:]
                sent_ref[:, at] = total[:half].astype(bf16)

    return pl.pallas_call(
        kernel,
        in_specs=[anywhere] * 2,
        out_specs=[whole_vmem] * 2,
        out_shape=[
            pltpu.VMEM((half, width), f32),
            pltpu.VMEM((half, width), bf16),
        ],
        scratch_shapes=[
            pltpu.VMEM((2, tokens, piece), bf16),
            pltpu.VMEM((depth, 2, cols, piece), bf16),
            pltpu.SemaphoreType.DMA((depth + 1,)),
        ],
        compiler_params=limits(24),
        cost_estimate=pl.CostEstimate(
            flops=4 * tokens * width * piece, bytes_accessed=4 * width * piece, transcendentals=0
        ),
        name="hidden_share",
    )(*in_hbm(gradient, pair))


def three_parts(value):
    high = lax.reduce_precision(value, 8, 7)
    rest = value - high
    middle = lax.reduce_precision(rest, 8, 7)
    return high, middle, rest - middle


def share_out(kept, arrived, found):
    rows, width = kept.shape
    count = lax.axis_size("ba")
    few = rows // count
    if few % 16:
        order = lax.axis_index("ba") ^ jnp.arange(count)
        summed = (kept + arrived.astype(f32)).astype(bf16).reshape(count, few, width)
        parts = jnp.stack(three_parts(jnp.sum(found))).astype(bf16)
        carried = jnp.zeros((few, lanes), bf16).at[0, :3].set(parts)
        return [jnp.concatenate([summed[order[s]], carried], axis=1) for s in range(count)]

    def kernel(kept_ref, arrived_ref, found_ref, *outs):
        me = lax.axis_index("ba")
        total = jnp.sum(found_ref[...], axis=0, keepdims=True)
        total = jnp.sum(total, axis=1, keepdims=True)
        high = total.astype(bf16).astype(f32)
        middle = (total - high).astype(bf16).astype(f32)
        low = total - high - middle
        lane = lax.broadcasted_iota(jnp.int32, (few, lanes), 1)
        lane = lane + lanes * lax.broadcasted_iota(jnp.int32, (few, lanes), 0)
        carried = jnp.where(lane == 0, high, jnp.where(lane == 1, middle, jnp.where(lane == 2, low, 0.0)))
        for s in range(count):
            at = pl.ds(pl.multiple_of((me ^ s) * few, few), few)
            outs[s][:, :width] = (kept_ref[at] + arrived_ref[at].astype(f32)).astype(bf16)
            outs[s][:, width:] = carried.astype(bf16)

    return pl.pallas_call(
        kernel,
        in_specs=[whole_vmem] * 3,
        out_specs=[whole_vmem] * count,
        out_shape=[jax.ShapeDtypeStruct((few, width + lanes), bf16)] * count,
        compiler_params=limits(20),
        name="share_out",
    )(in_vmem(kept), in_vmem(arrived), found)


def put_together(even, odd, few):
    rows, width = even.shape
    count = rows // few
    if few % 16:
        mine = lax.axis_index("ba") ^ jnp.arange(2 * count)
        both = jnp.stack([even.reshape(count, few, width), odd.reshape(count, few, width)], axis=1)
        return both.reshape(2 * count, few, width)[mine].reshape(2 * rows, width)

    def kernel(even_ref, odd_ref, out_ref, sem):
        me = lax.axis_index("ba")

        def place(s):
            to = pl.ds(pl.multiple_of((me ^ s) * few, few), few)
            ref = (even_ref, odd_ref)[s % 2]
            return pltpu.make_async_copy(ref.at[pl.ds(s // 2 * few, few)], out_ref.at[to], sem.at[s])

        for s in range(2 * count):
            place(s).start()
        for s in range(2 * count):
            place(s).wait()

    return pl.pallas_call(
        kernel,
        in_specs=[anywhere] * 2,
        out_specs=anywhere,
        out_shape=pltpu.HBM((2 * rows, width), bf16),
        scratch_shapes=[pltpu.SemaphoreType.DMA((2 * count,))],
        compiler_params=limits(4),
        name="put_together",
    )(even, odd)


def turn_features(hiddens):
    rows, width = hiddens[0].shape
    blocks = len(hiddens)
    tokens = rows * blocks
    share = width // blocks

    def kernel(*refs):
        given = refs[:blocks]
        left, held, sem = refs[blocks:]
        me = lax.axis_index("aa")

        def place(q):
            block = q // 2 * 2 + ((me % 2) ^ (q % 2))
            at = pl.ds(pl.multiple_of(block * rows, rows), rows)
            part = pl.ds(pl.multiple_of(me * share, share), share)
            return pltpu.make_async_copy(given[q].at[:, part], held.at[at], sem.at[q])

        for q in range(blocks):
            place(q).start()
        for q in range(blocks):
            place(q).wait()
        row = lax.broadcasted_iota(jnp.int32, (lanes, lanes), 0)
        col = lax.broadcasted_iota(jnp.int32, (lanes, lanes), 1)
        same = (row == col).astype(f32).astype(bf16)
        for d in range(0, share, lanes):
            left[d : d + lanes] = lax.dot_general(
                same, held[:, d : d + lanes], (((1,), (1,)), ((), ())), preferred_element_type=f32
            ).astype(bf16)

    return pl.pallas_call(
        kernel,
        in_specs=[anywhere] * blocks,
        out_specs=whole_vmem,
        out_shape=jax.ShapeDtypeStruct((share, tokens), bf16),
        scratch_shapes=[
            pltpu.VMEM((tokens, share), bf16),
            pltpu.SemaphoreType.DMA((blocks,)),
        ],
        compiler_params=limits(20),
        name="turn_features",
    )(*in_hbm(*hiddens))


def head_pair(left, own, other, partner, so_far):
    share, tokens = left.shape
    piece = own.shape[2]
    cols = largest_tile(piece, 512, lanes)
    part = largest_tile(cols, 256, lanes)
    steps = piece // cols
    aliased = [] if so_far is None else [so_far]

    def kernel(left_ref, own_ref, other_ref, *refs):
        out_ref, mixed, ready, out_sem = refs[len(aliased) :]
        step = pl.program_id(0)
        slot = lax.rem(step, 2)
        base = 2 * (my_pair() ^ partner)

        def store(k, s):
            at = pl.ds(pl.multiple_of(k * cols, cols), cols)
            return pltpu.make_async_copy(
                ready.at[s], out_ref.at[:, 0, pl.ds(base, 2), at], out_sem.at[s]
            )

        @pl.when(step >= 2)
        def _():
            store(step - 2, slot).wait()

        def unload(start):
            for n in range(start // lanes, (start + part) // lanes):
                ready[slot, :, :, n * lanes : (n + 1) * lanes] = (
                    mixed[n].astype(bf16).reshape(share, 2, lanes)
                )

        for j in range(0, cols, part):
            for i in range(2):
                right = jnp.concatenate(
                    [own_ref[i, :, j : j + part], other_ref[i, :, j : j + part]], axis=0
                )
                made = jnp.dot(left_ref[...], right, preferred_element_type=f32)
                for n in range(part // lanes):
                    mixed[j // lanes + n, pl.ds(i, share, stride=2), :] = made[
                        :, n * lanes : (n + 1) * lanes
                    ]
            if j:
                unload(j - part)
        unload(cols - part)
        store(step, slot).start()

        @pl.when(step == steps - 1)
        def _():
            if steps > 1:
                store(step - 1, 1 - slot).wait()
            store(step, slot).wait()

    return pl.pallas_call(
        kernel,
        grid=(steps,),
        in_specs=[whole_vmem]
        + [pl.BlockSpec((2, tokens // 2, cols), lambda r: (0, 0, r))] * 2
        + [anywhere] * len(aliased),
        out_specs=anywhere,
        out_shape=jax.ShapeDtypeStruct((share, 1, 4, piece), bf16),
        scratch_shapes=[
            pltpu.VMEM((cols // lanes, 2 * share, lanes), f32),
            pltpu.VMEM((2, share, 2, cols), bf16),
            pltpu.SemaphoreType.DMA((2,)),
        ],
        input_output_aliases={3: 0} if aliased else {},
        compiler_params=limits(30),
        cost_estimate=pl.CostEstimate(
            flops=4 * share * tokens * piece, bytes_accessed=4 * share * piece, transcendentals=0
        ),
        name="head_pair",
    )(left, *in_hbm(own, other), *aliased)


def on_device(hidden, head_weight, teacher):
    me_a = lax.axis_index("aa")
    me_b = lax.axis_index("ba")
    count = lax.axis_size("ba")
    near = count // 2
    few = teacher.shape[0]
    width = hidden.shape[1]
    tokens = few * count
    chip, core = me_a // 2, me_a % 2

    side = exchange(hidden, "aa", 2)
    beside = exchange(hidden, "aa", 1)
    *blocks, teacher_stat = split_teacher(teacher)
    blocks, beside, head_weight = lax.optimization_barrier((blocks, beside, head_weight))
    middle = near + 1
    queue = [*range(near - 1), near, near + 1, near - 1, *range(near + 2, count)]
    arrived = [exchange(blocks[s], "ba", s) if s else blocks[s] for s in queue[:middle]]
    pair = take_pair(head_weight)
    arrived[0], teacher_stat, late, side, pair = lax.optimization_barrier(
        (arrived[0], teacher_stat, [blocks[s] for s in queue[middle:]], side, pair)
    )
    hiddens = [hidden, beside, side, exchange(side, "aa", 1)]
    arrived += [exchange(block, "ba", s) for block, s in zip(late, queue[middle:])]
    teacher_stats = [teacher_stat, exchange(teacher_stat, "aa", 2)]

    def cross(parts):
        mine = join(parts)
        return [mine, exchange(mine, "aa", 2)]

    def swap(group):
        return group + [exchange(part, "aa", 1) for part in group]

    group_own = cross(arrived[:1])
    arrived[1:middle], group_own, pair = lax.optimization_barrier(
        (arrived[1:middle], group_own, pair)
    )
    group_a = cross(arrived[1:middle])
    student, student_stat = student_logits(hiddens, pair)
    arrived[middle:], student_stat = lax.optimization_barrier((arrived[middle:], student_stat))
    packed = pack_stats([student_stat], teacher_stats)
    group_a, packed = lax.optimization_barrier((group_a, packed))
    group_own, group_a = swap(group_own), swap(group_a)
    group_b = cross(arrived[middle:])
    packed = merge_two(packed, exchange(packed, "aa", 1))
    mask = 1
    while 2 * mask < count:
        met = exchange(packed, "ba", mask)
        if mask == 1:
            left = turn_features(hiddens)
            left, met = lax.optimization_barrier((left, met))
        packed = merge_two(packed, met)
        mask *= 2
    group_own, group_a, packed = lax.optimization_barrier((group_own, group_a, packed))
    sums = all_log_sums(packed, exchange(packed, "ba", mask))
    group_b, sums = lax.optimization_barrier((group_b, sums))
    groups = [group_own, group_a, swap(group_b)]

    order = [queue.index(s) for s in range(count)]
    bounds = [0, 1, middle]
    kinds = [int(n >= 1) + int(n >= middle) for n in order]
    table = [n - bounds[kind] for n, kind in zip(order, kinds)] + kinds

    def plan(group):
        here = jnp.stack([near * group, me_b, core]).astype(jnp.int32)
        return jnp.concatenate([here, jnp.array(table, jnp.int32)])

    grad_own, found = logit_gradient(plan(chip), groups, student, *sums)
    kept, sent = hidden_share(grad_own, pair)
    shares = share_out(kept, exchange(sent, "aa", 1), found)
    own_met = exchange(grad_own, "aa", 1)
    sums, own_met, shares = lax.optimization_barrier((sums, own_met, shares))
    grad_other, _ = logit_gradient(plan(1 - chip), groups, student, *sums)
    reduced = [exchange(shares[s], "ba", s) for s in range(1, count)]
    reduced, grad_other = lax.optimization_barrier((reduced, grad_other))
    summed = shares[0].astype(f32)
    for part in reduced:
        summed = summed + part.astype(f32)
    divergence = jnp.sum(summed[:, width:])[None] / tokens
    summed = summed[:, :width].astype(bf16)

    other_met = exchange(grad_other, "aa", 1)
    divergence = divergence + exchange(divergence, "aa", 1)
    gathered = [summed] + [exchange(summed, "ba", s) for s in range(2, count, 2)]
    grad_own, gathered[0] = lax.optimization_barrier((grad_own, gathered[0]))
    grad_head = head_pair(left, grad_own, grad_other, 0, None)
    gathered, grad_head, divergence, other_met = lax.optimization_barrier(
        (gathered, grad_head, divergence, other_met)
    )
    even = join(gathered)
    odd = exchange(even, "ba", 1)
    divergence = divergence + exchange(divergence, "aa", 2)
    even, other_met = lax.optimization_barrier((even, other_met))
    grad_head = head_pair(left, own_met, other_met, 1, grad_head)
    odd, grad_head = lax.optimization_barrier((odd, grad_head))
    grad_hidden = put_together(even, odd, summed.shape[0])
    return divergence[0], grad_hidden, grad_head


def solution(mesh):
    placed = (P("aa", None), P(None, "ba", None, None), P("ba", "aa", None, None))
    return jax.shard_map(
        on_device,
        mesh=mesh,
        in_specs=placed,
        out_specs=(P(), P("aa", None), P("aa", "ba", None, None)),
        check_vma=False,
    )
```

```python
import functools

import jax
import jax.numpy as jnp
from jax import lax
from jax.experimental import pallas as pl
from jax.experimental.pallas import tpu as pltpu
from jax.sharding import PartitionSpec as P

grad_scale = 256.0
lanes = 128
absent = -1e30
f32 = jnp.float32
bf16 = jnp.bfloat16
anywhere = pl.BlockSpec(memory_space=pl.ANY)
whole_vmem = pl.BlockSpec(memory_space=pltpu.VMEM)


def in_hbm(*values):
    return [pltpu.with_memory_space_constraint(value, pltpu.HBM) for value in values]


def in_vmem(value):
    return pltpu.with_memory_space_constraint(value, pltpu.VMEM)


def limits(mib):
    return pltpu.CompilerParams(vmem_limit_bytes=mib << 20)


def largest_tile(size, most, step):
    tile = min(size, most)
    while size % tile or tile % step:
        tile -= step
    return tile


def my_pair():
    me = lax.axis_index("aa")
    return (me % 2) ^ (me // 2)


def gate(values, deps):
    return lax.optimization_barrier((values, deps))[0]


def exchange(value, axis, mask):
    count = lax.axis_size(axis)
    return lax.ppermute(value, axis, [(i, i ^ mask) for i in range(count)])


def lane_row(column, rows):
    return jnp.transpose(jnp.broadcast_to(column, (rows, lanes)))[0:1]


def join(parts):
    starts = [sum(part.shape[0] for part in parts[:n]) for n in range(len(parts))]
    total = starts[-1] + parts[-1].shape[0]
    if len(parts) == 1:
        return parts[0]
    if any(part.shape[0] % 16 for part in parts):
        return jnp.concatenate(parts, axis=0)

    def kernel(*refs):
        given, (out_ref, sem) = refs[: len(parts)], refs[len(parts) :]
        copies = [
            pltpu.make_async_copy(ref, out_ref.at[pl.ds(start, ref.shape[0])], sem.at[n])
            for n, (ref, start) in enumerate(zip(given, starts))
        ]
        for copy in copies:
            copy.start()
        for copy in copies:
            copy.wait()

    return pl.pallas_call(
        kernel,
        in_specs=[anywhere] * len(parts),
        out_specs=anywhere,
        out_shape=pltpu.HBM((total, parts[0].shape[1]), bf16),
        scratch_shapes=[pltpu.SemaphoreType.DMA((len(parts),))],
        compiler_params=limits(4),
        name="join",
    )(*parts)


def split_teacher(teacher):
    tokens, _, owners, piece = teacher.shape
    every = tokens * owners
    cols = largest_tile(piece, 1024, lanes)

    def kernel(in_ref, *refs):
        outs, (stat_ref, peak_ref, total_ref) = refs[:owners], refs[owners:]
        step = pl.program_id(0)
        me = lax.axis_index("ba")
        flat = in_ref[:, 0].reshape(every, cols)
        row = lax.broadcasted_iota(jnp.int32, (every, every), 0)
        col = lax.broadcasted_iota(jnp.int32, (every, every), 1)
        source = (row % tokens) * owners + ((row // tokens) ^ me)
        pick = (col == source).astype(f32).astype(bf16)
        moved = jnp.dot(pick, flat, preferred_element_type=f32)
        for s in range(owners):
            outs[s][...] = moved[s * tokens : (s + 1) * tokens].astype(bf16)
        parts = [
            moved[s * tokens : (s + 1) * tokens, k : k + lanes]
            for s in range(owners)
            for k in range(0, cols, lanes)
        ]
        peak = functools.reduce(jnp.maximum, parts)

        @pl.when(step == 0)
        def _():
            peak_ref[...] = peak
            total_ref[...] = jnp.zeros_like(total_ref)

        old = peak_ref[...]
        new = jnp.maximum(old, peak)
        total = total_ref[...] * jnp.exp(old - new)
        for part in parts:
            total = total + jnp.exp(part - new)
        peak_ref[...] = new
        total_ref[...] = total

        @pl.when(step == pl.num_programs(0) - 1)
        def _():
            top = jnp.max(new, axis=1, keepdims=True)
            summed = jnp.sum(total * jnp.exp(new - top), axis=1, keepdims=True)
            token = lax.broadcasted_iota(jnp.int32, (tokens, every), 0) + me * tokens
            here = token == lax.broadcasted_iota(jnp.int32, (tokens, every), 1)
            peaks = jnp.max(jnp.where(here, top, absent), axis=0, keepdims=True)
            sums = jnp.sum(jnp.where(here, summed, 0.0), axis=0, keepdims=True)
            stat_ref[0:1, :] = peaks
            stat_ref[1:2, :] = sums
            stat_ref[2:8, :] = jnp.zeros((6, every), f32)

    return pl.pallas_call(
        kernel,
        grid=(piece // cols,),
        in_specs=[pl.BlockSpec((tokens, 1, owners, cols), lambda r: (0, 0, 0, r))],
        out_specs=[pl.BlockSpec((tokens, cols), lambda r: (0, r))] * owners
        + [pl.BlockSpec((8, every), lambda r: (0, 0))],
        out_shape=[pltpu.HBM((tokens, piece), bf16)] * owners
        + [jax.ShapeDtypeStruct((8, every), f32)],
        scratch_shapes=[pltpu.VMEM((tokens, lanes), f32)] * 2,
        compiler_params=limits(20),
        name="split_teacher",
    )(*in_hbm(teacher))


def take_pair(head_weight):
    width, _, _, piece = head_weight.shape
    rows = largest_tile(width, 256, lanes)
    steps = width // rows
    depth = min(4, steps)

    def kernel(w_ref, out_ref, taken, in_sem):
        pair = my_pair()
        row = lax.broadcasted_iota(jnp.int32, (2 * lanes, 2 * lanes), 0)
        col = lax.broadcasted_iota(jnp.int32, (2 * lanes, 2 * lanes), 1)
        pick = (col == (row % lanes) * 2 + row // lanes).astype(f32).astype(bf16)

        def fetch(i):
            return pltpu.make_async_copy(
                w_ref.at[pl.ds(i * rows, rows), 0, pl.ds(2 * pair, 2), :],
                taken.at[i % depth],
                in_sem.at[i % depth],
            )

        for i in range(depth):
            fetch(i).start()
        for i in range(steps):
            fetch(i).wait()
            for q in range(0, rows, lanes):
                block = taken[i % depth, q : q + lanes].reshape(2 * lanes, piece)
                moved = jnp.dot(pick, block, preferred_element_type=f32).astype(bf16)
                at = i * rows + q
                out_ref[0, at : at + lanes] = moved[:lanes]
                out_ref[1, at : at + lanes] = moved[lanes:]
            if i + depth < steps:
                fetch(i + depth).start()

    return pl.pallas_call(
        kernel,
        in_specs=[anywhere],
        out_specs=whole_vmem,
        out_shape=pltpu.VMEM((2, width, piece), bf16),
        scratch_shapes=[
            pltpu.VMEM((depth, rows, 2, piece), bf16),
            pltpu.SemaphoreType.DMA((depth,)),
        ],
        compiler_params=limits(20),
        cost_estimate=pl.CostEstimate(
            flops=16 * lanes * width * piece,
            bytes_accessed=4 * width * piece,
            transcendentals=0,
        ),
        name="take_pair",
    )(head_weight)


def student_logits(hiddens, pair):
    rows, width = hiddens[0].shape
    blocks = len(hiddens)
    tokens = rows * blocks
    piece = pair.shape[2]
    cols = largest_tile(piece, 1024, lanes)
    part = largest_tile(cols, 256, lanes)

    def kernel(*refs):
        given, w_ref = refs[:blocks], refs[blocks]
        out_ref, stat_ref, left, peak_ref, total_ref, sem = refs[blocks + 1 :]
        first = (pl.program_id(0) == 0) & (pl.program_id(1) == 0)
        last = (pl.program_id(0) == 1) & (pl.program_id(1) == pl.num_programs(1) - 1)
        me = lax.axis_index("aa")

        @pl.when(first)
        def _():
            def place(q):
                at = pl.ds(pl.multiple_of((me ^ q) * rows, rows), rows)
                return pltpu.make_async_copy(given[q], left.at[at], sem.at[q])

            for q in range(blocks):
                place(q).start()
            peak_ref[...] = jnp.full_like(peak_ref, absent)
            total_ref[...] = jnp.zeros_like(total_ref)
            for q in range(blocks):
                place(q).wait()

        def collect(start):
            for k in range(0, tokens, 64):
                at = pl.ds(k, 64)
                parts = [out_ref[0, at, j : j + lanes] for j in range(start, start + part, lanes)]
                old = peak_ref[at]
                new = functools.reduce(jnp.maximum, parts, old)
                total = total_ref[at] * jnp.exp(old - new)
                for value in parts:
                    total = total + jnp.exp(value - new)
                peak_ref[at] = new
                total_ref[at] = total

        for n in range(0, cols, part):
            at = pl.ds(pl.multiple_of(pl.program_id(1) * cols + n, part), part)
            out_ref[0, :, n : n + part] = jnp.dot(
                left[...], w_ref[pl.program_id(0), :, at], preferred_element_type=f32
            )
            if n:
                collect(n - part)
        collect(cols - part)

        @pl.when(last)
        def _():
            peak = peak_ref[...]
            top = jnp.max(peak, axis=1, keepdims=True)
            summed = jnp.sum(total_ref[...] * jnp.exp(peak - top), axis=1, keepdims=True)
            stat_ref[0:1, :] = lane_row(top, tokens)
            stat_ref[1:2, :] = lane_row(summed, tokens)
            stat_ref[2:8, :] = jnp.zeros((6, tokens), f32)

    return pl.pallas_call(
        kernel,
        grid=(2, piece // cols),
        in_specs=[anywhere] * blocks
        + [whole_vmem],
        out_specs=[
            pl.BlockSpec((1, tokens, cols), lambda i, r: (i, 0, r)),
            pl.BlockSpec((8, tokens), lambda i, r: (0, 0)),
        ],
        out_shape=[
            pltpu.HBM((2, tokens, piece), f32),
            jax.ShapeDtypeStruct((8, tokens), f32),
        ],
        scratch_shapes=[
            pltpu.VMEM((tokens, width), bf16),
            pltpu.VMEM((tokens, lanes), f32),
            pltpu.VMEM((tokens, lanes), f32),
            pltpu.SemaphoreType.DMA((blocks,)),
        ],
        compiler_params=limits(20),
        cost_estimate=pl.CostEstimate(flops=1, bytes_accessed=1, transcendentals=0),
        name="student_logits",
    )(*in_hbm(*hiddens), in_vmem(pair))


def merge(stats, row=0):
    peak = functools.reduce(jnp.maximum, [s[row : row + 1] for s in stats])
    total = sum(s[row + 1 : row + 2] * jnp.exp(s[row : row + 1] - peak) for s in stats)
    return peak, total


def pack_stats(student_stats, teacher_stats):
    tokens = student_stats[0].shape[1]
    count = len(student_stats)

    def kernel(*refs):
        out_ref = refs[-1]
        peak, total = merge([r[...] for r in refs[:count]])
        out_ref[0:1, :] = peak
        out_ref[1:2, :] = total
        peak, total = merge([r[...] for r in refs[count:-1]])
        out_ref[2:3, :] = peak
        out_ref[3:4, :] = total
        out_ref[4:8, :] = jnp.zeros((4, tokens), f32)

    return pl.pallas_call(
        kernel,
        in_specs=[whole_vmem] * (count + len(teacher_stats)),
        out_specs=whole_vmem,
        out_shape=jax.ShapeDtypeStruct((8, tokens), f32),
        compiler_params=limits(20),
        name="pack_stats",
    )(*student_stats, *teacher_stats)


def merge_two(first, second):
    tokens = first.shape[1]

    def kernel(a_ref, b_ref, out_ref):
        both = [a_ref[...], b_ref[...]]
        for row in (0, 2):
            peak, total = merge(both, row)
            out_ref[row : row + 1, :] = peak
            out_ref[row + 1 : row + 2, :] = total
        out_ref[4:8, :] = jnp.zeros((4, tokens), f32)

    return pl.pallas_call(
        kernel,
        in_specs=[whole_vmem] * 2,
        out_specs=whole_vmem,
        out_shape=jax.ShapeDtypeStruct((8, tokens), f32),
        compiler_params=limits(20),
        name="merge_two",
    )(first, second)


def all_log_sums(first, second):
    tokens = first.shape[1]

    def kernel(a_ref, b_ref, *outs):
        both = [a_ref[...], b_ref[...]]
        for row, out_ref in zip((0, 2), outs):
            peak, total = merge(both, row)
            wide = jnp.broadcast_to(peak + jnp.log(total), (lanes, tokens))
            out_ref[...] = jnp.transpose(wide)

    return pl.pallas_call(
        kernel,
        in_specs=[whole_vmem] * 2,
        out_specs=[whole_vmem] * 2,
        out_shape=[pltpu.HBM((tokens, lanes), f32)] * 2,
        compiler_params=limits(20),
        name="all_log_sums",
    )(first, second)


def logit_gradient(plan, groups, student, student_sum, teacher_sum):
    count = (plan.shape[0] - 3) // 2
    _, tokens, piece = student.shape
    half = tokens // 2
    few = tokens // count
    per = 2 if count // 2 % 2 == 0 else 1
    steps = count // 2 // per
    cols = largest_tile(piece, 512, lanes)
    rows = 16

    def kernel(plan_ref, *refs):
        teachers = [refs[4 * n : 4 * n + 4] for n in range(len(groups))]
        s_ref, ssum_ref, tsum_ref, g_ref, div_ref, held, sem = refs[4 * len(groups) :]
        step = pl.program_id(0)
        slot = lax.rem(step, 2)
        core = plan_ref[2]

        def fetch(k, to):
            for m in range(per):
                s = (plan_ref[0] + k * per + m) ^ plan_ref[1]
                block = pl.ds(pl.multiple_of(plan_ref[3 + s] * few, few), few)
                for n, (own, side, own_met, side_met) in enumerate(teachers):
                    for at_core, ordered in enumerate(((own, own_met), (side_met, side))):

                        @pl.when((plan_ref[3 + count + s] == n) & (core == at_core))
                        def _(ordered=ordered, block=block, m=m):
                            for i in range(2):
                                pltpu.make_async_copy(
                                    ordered[i].at[block],
                                    held.at[to, i, pl.ds(m * few, few)],
                                    sem.at[to, i, m],
                                ).start()

        @pl.when(step == 0)
        def _():
            div_ref[...] = jnp.zeros_like(div_ref)
            fetch(0, 0)

        @pl.when(step + 1 < steps)
        def _():
            fetch(step + 1, 1 - slot)

        for i in range(2):
            for m in range(per):
                pltpu.make_async_copy(
                    teachers[0][0].at[pl.ds(0, few)],
                    held.at[slot, i, pl.ds(m * few, few)],
                    sem.at[slot, i, m],
                ).wait()

        @pl.loop(0, per * few // rows)
        def _(k):
            at = pl.ds(pl.multiple_of(k * rows, rows), rows)
            ssum = jnp.concatenate([ssum_ref[at]] * (cols // lanes), axis=1)
            tsum = jnp.concatenate([tsum_ref[at]] * (cols // lanes), axis=1)
            found = jnp.zeros((rows, cols), f32)
            for i in range(2):
                for j in range(0, piece, cols):
                    log_s = s_ref[i, at, j : j + cols] - ssum
                    log_t = held[slot, i, at, j : j + cols].astype(f32) - tsum
                    prob_t = jnp.exp(log_t)
                    g_ref[i, at, j : j + cols] = (
                        grad_scale * (jnp.exp(log_s) - prob_t)
                    ).astype(bf16)
                    found = found + prob_t * (log_t - log_s)
            folded = [
                found[m : m + 8, n : n + lanes]
                for m in range(0, rows, 8)
                for n in range(0, cols, lanes)
            ]
            div_ref[...] += sum(folded[1:], folded[0])

    return pl.pallas_call(
        kernel,
        grid_spec=pltpu.PrefetchScalarGridSpec(
            num_scalar_prefetch=1,
            grid=(steps,),
            in_specs=[anywhere] * (4 * len(groups))
            + [pl.BlockSpec((2, per * few, piece), lambda s, p: (0, p[0] // per + s, 0))]
            + [pl.BlockSpec((per * few, lanes), lambda s, p: (p[0] // per + s, 0))] * 2,
            out_specs=[
                pl.BlockSpec((2, per * few, piece), lambda s, p: (0, s, 0)),
                pl.BlockSpec((8, lanes), lambda s, p: (0, 0)),
            ],
            scratch_shapes=[
                pltpu.VMEM((2, 2, per * few, piece), bf16),
                pltpu.SemaphoreType.DMA((2, 2, per)),
            ],
        ),
        out_shape=[
            pltpu.HBM((2, half, piece), bf16),
            jax.ShapeDtypeStruct((8, lanes), f32),
        ],
        compiler_params=limits(20),
        cost_estimate=pl.CostEstimate(
            flops=8 * half * piece, bytes_accessed=16 * half * piece, transcendentals=4 * half * piece
        ),
        name="logit_gradient",
    )(
        plan,
        *in_hbm(*[part for group in groups for part in group]),
        *in_hbm(student, student_sum, teacher_sum),
    )


def hidden_share(gradient, pair):
    _, tokens, piece = gradient.shape
    width = pair.shape[1]
    half = tokens // 2
    cols = largest_tile(width, 512, lanes)
    steps = width // cols
    depth = min(3, steps)

    def kernel(given_ref, w_ref, kept_ref, sent_ref, g_ref, taken, sem):
        core = lax.axis_index("aa") % 2

        def fetch(k):
            at = pl.ds(k * cols, cols)
            return pltpu.make_async_copy(w_ref.at[:, at, :], taken.at[k % depth], sem.at[k % depth])

        load = pltpu.make_async_copy(given_ref, g_ref, sem.at[depth])
        load.start()
        for k in range(depth):
            fetch(k).start()
        load.wait()
        for k in range(steps):
            fetch(k).wait()
            total = sum(
                lax.dot_general(
                    g_ref[i],
                    taken[k % depth, i],
                    (((1,), (1,)), ((), ())),
                    preferred_element_type=f32,
                )
                for i in range(2)
            )
            if k + depth < steps:
                fetch(k + depth).start()
            at = slice(k * cols, (k + 1) * cols)

            @pl.when(core == 0)
            def _(total=total, at=at):
                kept_ref[:, at] = total[:half]
                sent_ref[:, at] = total[half:].astype(bf16)

            @pl.when(core == 1)
            def _(total=total, at=at):
                kept_ref[:, at] = total[half:]
                sent_ref[:, at] = total[:half].astype(bf16)

    return pl.pallas_call(
        kernel,
        in_specs=[anywhere] * 2,
        out_specs=[whole_vmem] * 2,
        out_shape=[
            pltpu.VMEM((half, width), f32),
            pltpu.VMEM((half, width), bf16),
        ],
        scratch_shapes=[
            pltpu.VMEM((2, tokens, piece), bf16),
            pltpu.VMEM((depth, 2, cols, piece), bf16),
            pltpu.SemaphoreType.DMA((depth + 1,)),
        ],
        compiler_params=limits(24),
        cost_estimate=pl.CostEstimate(
            flops=4 * tokens * width * piece, bytes_accessed=4 * width * piece, transcendentals=0
        ),
        name="hidden_share",
    )(*in_hbm(gradient, pair))


def three_parts(value):
    high = lax.reduce_precision(value, 8, 7)
    rest = value - high
    middle = lax.reduce_precision(rest, 8, 7)
    return high, middle, rest - middle


def share_out(kept, arrived, found):
    rows, width = kept.shape
    count = lax.axis_size("ba")
    few = rows // count
    if few % 16:
        order = lax.axis_index("ba") ^ jnp.arange(count)
        summed = (kept + arrived.astype(f32)).astype(bf16).reshape(count, few, width)
        parts = jnp.stack(three_parts(jnp.sum(found))).astype(bf16)
        carried = jnp.zeros((few, lanes), bf16).at[0, :3].set(parts)
        return [jnp.concatenate([summed[order[s]], carried], axis=1) for s in range(count)]

    def kernel(kept_ref, arrived_ref, found_ref, *outs):
        me = lax.axis_index("ba")
        total = jnp.sum(found_ref[...], axis=0, keepdims=True)
        total = jnp.sum(total, axis=1, keepdims=True)
        high = total.astype(bf16).astype(f32)
        middle = (total - high).astype(bf16).astype(f32)
        low = total - high - middle
        lane = lax.broadcasted_iota(jnp.int32, (few, lanes), 1)
        lane = lane + lanes * lax.broadcasted_iota(jnp.int32, (few, lanes), 0)
        carried = jnp.where(lane == 0, high, jnp.where(lane == 1, middle, jnp.where(lane == 2, low, 0.0)))
        for s in range(count):
            at = pl.ds(pl.multiple_of((me ^ s) * few, few), few)
            outs[s][:, :width] = (kept_ref[at] + arrived_ref[at].astype(f32)).astype(bf16)
            outs[s][:, width:] = carried.astype(bf16)

    return pl.pallas_call(
        kernel,
        in_specs=[whole_vmem] * 3,
        out_specs=[whole_vmem] * count,
        out_shape=[jax.ShapeDtypeStruct((few, width + lanes), bf16)] * count,
        compiler_params=limits(20),
        name="share_out",
    )(in_vmem(kept), in_vmem(arrived), found)


def put_together(even, odd, few):
    rows, width = even.shape
    count = rows // few
    if few % 16:
        mine = lax.axis_index("ba") ^ jnp.arange(2 * count)
        both = jnp.stack([even.reshape(count, few, width), odd.reshape(count, few, width)], axis=1)
        return both.reshape(2 * count, few, width)[mine].reshape(2 * rows, width)

    def kernel(even_ref, odd_ref, out_ref, sem):
        me = lax.axis_index("ba")

        def place(s):
            to = pl.ds(pl.multiple_of((me ^ s) * few, few), few)
            ref = (even_ref, odd_ref)[s % 2]
            return pltpu.make_async_copy(ref.at[pl.ds(s // 2 * few, few)], out_ref.at[to], sem.at[s])

        for s in range(2 * count):
            place(s).start()
        for s in range(2 * count):
            place(s).wait()

    return pl.pallas_call(
        kernel,
        in_specs=[anywhere] * 2,
        out_specs=anywhere,
        out_shape=pltpu.HBM((2 * rows, width), bf16),
        scratch_shapes=[pltpu.SemaphoreType.DMA((2 * count,))],
        compiler_params=limits(4),
        name="put_together",
    )(even, odd)


def turn_features(hiddens):
    rows, width = hiddens[0].shape
    blocks = len(hiddens)
    tokens = rows * blocks
    share = width // blocks

    def kernel(*refs):
        given = refs[:blocks]
        left, held, sem = refs[blocks:]
        me = lax.axis_index("aa")

        def place(q):
            block = q // 2 * 2 + ((me % 2) ^ (q % 2))
            at = pl.ds(pl.multiple_of(block * rows, rows), rows)
            part = pl.ds(pl.multiple_of(me * share, share), share)
            return pltpu.make_async_copy(given[q].at[:, part], held.at[at], sem.at[q])

        for q in range(blocks):
            place(q).start()
        for q in range(blocks):
            place(q).wait()
        row = lax.broadcasted_iota(jnp.int32, (lanes, lanes), 0)
        col = lax.broadcasted_iota(jnp.int32, (lanes, lanes), 1)
        same = (row == col).astype(f32).astype(bf16)
        for d in range(0, share, lanes):
            left[d : d + lanes] = lax.dot_general(
                same, held[:, d : d + lanes], (((1,), (1,)), ((), ())), preferred_element_type=f32
            ).astype(bf16)

    return pl.pallas_call(
        kernel,
        in_specs=[anywhere] * blocks,
        out_specs=whole_vmem,
        out_shape=jax.ShapeDtypeStruct((share, tokens), bf16),
        scratch_shapes=[
            pltpu.VMEM((tokens, share), bf16),
            pltpu.SemaphoreType.DMA((blocks,)),
        ],
        compiler_params=limits(20),
        name="turn_features",
    )(*in_hbm(*hiddens))


def head_pair(left, own, other, partner, so_far):
    share, tokens = left.shape
    piece = own.shape[2]
    cols = largest_tile(piece, 512, lanes)
    part = largest_tile(cols, 256, lanes)
    steps = piece // cols
    aliased = [] if so_far is None else [so_far]

    def kernel(left_ref, own_ref, other_ref, *refs):
        out_ref, mixed, ready, out_sem = refs[len(aliased) :]
        step = pl.program_id(0)
        slot = lax.rem(step, 2)
        base = 2 * (my_pair() ^ partner)

        def store(k, s):
            at = pl.ds(pl.multiple_of(k * cols, cols), cols)
            return pltpu.make_async_copy(
                ready.at[s], out_ref.at[:, 0, pl.ds(base, 2), at], out_sem.at[s]
            )

        @pl.when(step >= 2)
        def _():
            store(step - 2, slot).wait()

        def unload(start):
            for n in range(start // lanes, (start + part) // lanes):
                ready[slot, :, :, n * lanes : (n + 1) * lanes] = (
                    mixed[n].astype(bf16).reshape(share, 2, lanes)
                )

        for j in range(0, cols, part):
            for i in range(2):
                right = jnp.concatenate(
                    [own_ref[i, :, j : j + part], other_ref[i, :, j : j + part]], axis=0
                )
                made = jnp.dot(left_ref[...], right, preferred_element_type=f32)
                for n in range(part // lanes):
                    mixed[j // lanes + n, pl.ds(i, share, stride=2), :] = made[
                        :, n * lanes : (n + 1) * lanes
                    ]
            if j:
                unload(j - part)
        unload(cols - part)
        store(step, slot).start()

        @pl.when(step == steps - 1)
        def _():
            if steps > 1:
                store(step - 1, 1 - slot).wait()
            store(step, slot).wait()

    return pl.pallas_call(
        kernel,
        grid=(steps,),
        in_specs=[whole_vmem]
        + [pl.BlockSpec((2, tokens // 2, cols), lambda r: (0, 0, r))] * 2
        + [anywhere] * len(aliased),
        out_specs=anywhere,
        out_shape=jax.ShapeDtypeStruct((share, 1, 4, piece), bf16),
        scratch_shapes=[
            pltpu.VMEM((cols // lanes, 2 * share, lanes), f32),
            pltpu.VMEM((2, share, 2, cols), bf16),
            pltpu.SemaphoreType.DMA((2,)),
        ],
        input_output_aliases={3: 0} if aliased else {},
        compiler_params=limits(30),
        cost_estimate=pl.CostEstimate(
            flops=4 * share * tokens * piece, bytes_accessed=4 * share * piece, transcendentals=0
        ),
        name="head_pair",
    )(left, *in_hbm(own, other), *aliased)


def on_device(hidden, head_weight, teacher):
    me_a = lax.axis_index("aa")
    me_b = lax.axis_index("ba")
    count = lax.axis_size("ba")
    near = count // 2
    few = teacher.shape[0]
    width = hidden.shape[1]
    tokens = few * count
    chip, core = me_a // 2, me_a % 2

    side = exchange(hidden, "aa", 2)
    beside = exchange(hidden, "aa", 1)
    *blocks, teacher_stat = split_teacher(teacher)
    blocks, beside, head_weight = lax.optimization_barrier((blocks, beside, head_weight))
    middle = near + 1
    queue = [*range(near - 1), near, near + 1, near - 1, *range(near + 2, count)]
    arrived = [exchange(blocks[s], "ba", s) if s else blocks[s] for s in queue[:middle]]
    pair = take_pair(head_weight)
    arrived[0], teacher_stat, late, side, pair = lax.optimization_barrier(
        (arrived[0], teacher_stat, [blocks[s] for s in queue[middle:]], side, pair)
    )
    hiddens = [hidden, beside, side, exchange(side, "aa", 1)]
    arrived += [exchange(block, "ba", s) for block, s in zip(late, queue[middle:])]
    teacher_stats = [teacher_stat, exchange(teacher_stat, "aa", 2)]

    def cross(parts):
        mine = join(parts)
        return [mine, exchange(mine, "aa", 2)]

    def swap(group):
        return group + [exchange(part, "aa", 1) for part in group]

    group_own = cross(arrived[:1])
    arrived[1:middle], group_own, pair = lax.optimization_barrier(
        (arrived[1:middle], group_own, pair)
    )
    group_a = cross(arrived[1:middle])
    student, student_stat = student_logits(hiddens, pair)
    arrived[middle:], student_stat = lax.optimization_barrier((arrived[middle:], student_stat))
    packed = pack_stats([student_stat], teacher_stats)
    group_a, packed = lax.optimization_barrier((group_a, packed))
    group_own, group_a = swap(group_own), swap(group_a)
    group_b = cross(arrived[middle:])
    packed = merge_two(packed, exchange(packed, "aa", 1))
    mask = 1
    while 2 * mask < count:
        met = exchange(packed, "ba", mask)
        if mask == 1:
            left = turn_features(hiddens)
            left, met = lax.optimization_barrier((left, met))
        packed = merge_two(packed, met)
        mask *= 2
    group_own, group_a, packed = lax.optimization_barrier((group_own, group_a, packed))
    sums = all_log_sums(packed, exchange(packed, "ba", mask))
    group_b, sums = lax.optimization_barrier((group_b, sums))
    groups = [group_own, group_a, swap(group_b)]

    order = [queue.index(s) for s in range(count)]
    bounds = [0, 1, middle]
    kinds = [int(n >= 1) + int(n >= middle) for n in order]
    table = [n - bounds[kind] for n, kind in zip(order, kinds)] + kinds

    def plan(group):
        here = jnp.stack([near * group, me_b, core]).astype(jnp.int32)
        return jnp.concatenate([here, jnp.array(table, jnp.int32)])

    grad_own, found = logit_gradient(plan(chip), groups, student, *sums)
    kept, sent = hidden_share(grad_own, pair)
    shares = share_out(kept, exchange(sent, "aa", 1), found)
    own_met = exchange(grad_own, "aa", 1)
    sums, own_met, shares = lax.optimization_barrier((sums, own_met, shares))
    grad_other, _ = logit_gradient(plan(1 - chip), groups, student, *sums)
    reduced = [exchange(shares[s], "ba", s) for s in range(1, count)]
    reduced, grad_other = lax.optimization_barrier((reduced, grad_other))
    summed = shares[0].astype(f32)
    for part in reduced:
        summed = summed + part.astype(f32)
    divergence = jnp.sum(summed[:, width:])[None] / tokens
    summed = summed[:, :width].astype(bf16)

    other_met = exchange(grad_other, "aa", 1)
    gathered = [summed] + [exchange(summed, "ba", s) for s in range(2, count, 2)]
    grad_own, gathered[0] = lax.optimization_barrier((grad_own, gathered[0]))
    grad_head = head_pair(left, grad_own, grad_other, 0, None)
    gathered, grad_head, divergence, other_met = lax.optimization_barrier(
        (gathered, grad_head, divergence, other_met)
    )
    even = join(gathered)
    odd = exchange(even, "ba", 1)
    beside, side, across = [exchange(divergence, "aa", m) for m in (1, 2, 3)]
    even, other_met = lax.optimization_barrier((even, other_met))
    grad_head = head_pair(left, own_met, other_met, 1, grad_head)
    odd, grad_head = lax.optimization_barrier((odd, grad_head))
    grad_hidden = put_together(even, odd, summed.shape[0])
    divergence = (divergence + beside) + (side + across)
    return divergence[0], grad_hidden, grad_head


def solution(mesh):
    placed = (P("aa", None), P(None, "ba", None, None), P("ba", "aa", None, None))
    return jax.shard_map(
        on_device,
        mesh=mesh,
        in_specs=placed,
        out_specs=(P(), P("aa", None), P("aa", "ba", None, None)),
        check_vma=False,
    )
```
